32 devices in a mesh: mem: 8 (over y, x, core), lat: 4 (over z).
Axes of the slice: x: 2, y: 2, z: 4, core: 2. Of those that a mesh axis runs over, the one named last changes fastest.
Arguments:
- members: bfloat16 [80, 2, 4, 32, 1152], P('mem', None, None, 'lat'), may hold values from -0.625 to 0.625
- alpha: float32 [80, 4, 32, 1152], P('mem', None, 'lat'), may hold values from -6 to 6
- zonal_loc: bfloat16 [1152, 1152], replicated
- merid_coef: float32 [32, 9], replicated, may hold values from 0.1 to 0.6
- slot_tile: int32 [4, 8, 3], P('lat', 'mem'), may hold values from 0 to 17, as said below
- obs_count: int32 [4, 8, 3], P('lat', 'mem'), may hold values from 0 to 4096, as said below
- obs_index: int32 [4, 8, 3, 4096], P('lat', 'mem'), may hold values from 0 to 16383
- obs_value: float32 [4, 8, 3, 4096], P('lat', 'mem'), may hold values from -6 to 6
- obs_weight: float32 [4, 8, 3, 4096], P('lat', 'mem'), may hold values from 0.5 to 4
Outputs:
- analysis_alpha: float32 [80, 4, 32, 1152], P('mem', None, 'lat')
The draws below stay inside these ranges and needn't reach their ends.
Inputs may be any that keep to these rules, and one draw needn't show every extreme that they name: `slot_tile`: within each band every tile 0..17 stands in exactly one slot; a device owns at most 3 tiles of a band, and in every band one device owns exactly 3. Unused slots hold tile 0. `obs_count`: zero exactly in unused slots; a used slot holds 4096, 2048 or 1024 live observations, and each band has a slot with 4096.
All inputs are finite; a program needn't handle non-finite values.
Results may differ from the reference program's by a relative error of at most 0.00065.
Values may be sent and summed in bfloat16 or wider, within the bound.
No kernel may reach another device: no remote copies, remote signals or barrier semaphores. Data moves between devices by JAX's collectives and lax.ppermute only.
A program may use at most 64 MiB of HBM per device.

```python
import math
import jax
import jax.numpy as jnp
from jax import lax

MEMBERS = 80
VARS = 2
LEV = 4
NLON = 1152
CLAT_DEV = 8
BAND = 4
TLON = 128
MAXOWN = 3
OBS_TILE = 4096
ITERS = 2
BANDS = 4
CLAT = 32
NTILE = 18
TILE_CELLS = 16384
N_MEM = 8


def draw_zonal_loc(key, part):
    columns = jnp.arange(NLON)
    distance = jnp.abs(columns[:, None] - columns[None, :])
    distance = jnp.minimum(distance, NLON - distance).astype(jnp.float32)
    length_scale = NLON / 4.0
    roughness = jax.random.uniform(key, (NLON, NLON), jnp.float32, 0.4, 1.6)
    off_diag = 0.035 * jnp.exp(-0.5 * (distance / length_scale) ** 2) * roughness
    return jnp.where(distance == 0, jnp.float32(1.0), off_diag).astype(jnp.bfloat16)


def ownership_band(band_key):
    tile_key, device_key, count_key = jax.random.split(band_key, 3)
    tile_perm = jax.random.permutation(tile_key, NTILE).astype(jnp.int32)
    device_perm = jax.random.permutation(device_key, N_MEM).astype(jnp.int32)
    position = jnp.arange(NTILE, dtype=jnp.int32)
    remainder = jnp.maximum(position - MAXOWN, 0)
    others = N_MEM - 1
    device = jnp.where(position < MAXOWN, device_perm[0], device_perm[1 + remainder % others])
    slot_place = jnp.where(position < MAXOWN, position, remainder // others)
    halvings = jax.random.randint(count_key, (NTILE,), 0, 3)
    live_counts = OBS_TILE // jnp.left_shift(jnp.int32(1), halvings.astype(jnp.int32))
    live_counts = jnp.where(position == 0, OBS_TILE, live_counts).astype(jnp.int32)
    tile_table = jnp.zeros((N_MEM, MAXOWN), jnp.int32).at[device, slot_place].set(tile_perm)
    count_table = jnp.zeros((N_MEM, MAXOWN), jnp.int32).at[device, slot_place].set(live_counts)
    return (tile_table, count_table)


def ownership(key):
    base_key = jax.random.fold_in(key, 7)
    band_keys = jax.random.split(base_key, BANDS)
    return jax.vmap(ownership_band)(band_keys)


def draw_slot_tile(key, part):
    return ownership(key)[0]


def draw_obs_count(key, part):
    return ownership(key)[1]


def place_ends(array, own_key, low, largest):
    longest = array.shape.index(max(array.shape))
    spots = []
    for shift in (0, 1):
        where = [jax.random.randint(jax.random.fold_in(own_key, axis), (), 0, length) for axis, length in enumerate(array.shape)]
        where[longest] = (where[longest] + shift) % array.shape[longest]
        spots.append(tuple(where))
    return array.at[spots[0]].set(low).at[spots[1]].set(largest)


def level_of(stream_key, shape, pieces, low, high):
    factor_of = 1.0
    for axis_at, blocks in pieces:
        steps = jax.random.uniform(jax.random.fold_in(jax.random.fold_in(stream_key, 6), axis_at), (blocks,), jnp.float32, low / len(pieces), high / len(pieces))
        factor_of = factor_of * jnp.repeat(jnp.exp(steps), shape[axis_at] // blocks).reshape((-1,) + (1,) * (len(shape) - 1 - axis_at))
    return factor_of


def scatter_about(stream_key, extent, scale, reach, cuts=(), kind=jnp.bfloat16):
    loudness = level_of(stream_key, extent, cuts, -0.22, 0.18) if cuts else 1.0
    array = jax.random.normal(stream_key, extent, jnp.float32) * scale * loudness
    return jnp.minimum(jnp.maximum(array, -reach), reach).astype(kind)


def setup_inputs(seed: int = 0) -> dict:
    splits = jax.random.split(jax.random.key(seed), 10)
    members = scatter_about(splits[0], (MEMBERS, VARS, LEV, CLAT, NLON), MEMBERS ** -0.5, 0.625, ((0, 8), (3, 4)))
    alpha = scatter_about(splits[1], (MEMBERS, LEV, CLAT, NLON), 1.0, 6.0, ((0, 8), (2, 4)), jnp.float32)
    zonal_loc = draw_zonal_loc(jax.random.fold_in(splits[9], 71), 0)
    merid_coef = jnp.clip(jax.random.uniform(splits[3], (CLAT, 2 * BAND + 1), jnp.float32, 0.1, 0.6), 0.1, 0.6)
    slot_tile = draw_slot_tile(jax.random.fold_in(splits[9], 71), 0)
    obs_count = draw_obs_count(jax.random.fold_in(splits[9], 71), 0)
    obs_index = place_ends(jax.random.randint(splits[6], (BANDS, N_MEM, MAXOWN, OBS_TILE), 0, TILE_CELLS), jax.random.fold_in(splits[6], 1), 0, TILE_CELLS - 1).astype(jnp.int32)
    obs_value = scatter_about(splits[7], (BANDS, N_MEM, MAXOWN, OBS_TILE), 1.0, 6.0, ((0, 4), (1, 8)), jnp.float32)
    obs_weight = jnp.clip(jnp.exp(math.log(4.0) - 2.0794415 * jax.random.uniform(splits[8], (BANDS, N_MEM, MAXOWN, OBS_TILE), jnp.float32) ** level_of(splits[8], (BANDS, N_MEM, MAXOWN, OBS_TILE), ((0, 4), (1, 8)), -0.2, 0.2)), 0.5, 4.0)
    return dict(members=members, alpha=alpha, zonal_loc=zonal_loc, merid_coef=merid_coef, slot_tile=slot_tile, obs_count=obs_count, obs_index=obs_index, obs_value=obs_value, obs_weight=obs_weight)


step_size = 0.3

def localize(member_alpha, merid_coef, zonal_loc):
    alpha_pad = jnp.pad(member_alpha, ((0, 0), (BAND, BAND), (0, 0)))
    running = jnp.zeros(member_alpha.shape, jnp.float32)
    for offset in range(-BAND, BAND + 1):
        running = running + merid_coef[:, offset + BAND][None, :, None] * alpha_pad[:, BAND + offset:BAND + offset + CLAT]
    spread = running.astype(jnp.bfloat16)
    zonal_out = jnp.dot(spread.reshape(-1, NLON), zonal_loc, preferred_element_type=jnp.float32)
    return zonal_out.reshape(member_alpha.shape)

def meridional_back(zonal_back, merid_coef):
    back_pad = jnp.pad(zonal_back, ((0, 0), (BAND, BAND), (0, 0)))
    coef_pad = jnp.pad(merid_coef, ((BAND, BAND), (0, 0)))
    running = jnp.zeros(zonal_back.shape, jnp.float32)
    for offset in range(-BAND, BAND + 1):
        running = running + coef_pad[BAND - offset:BAND - offset + CLAT, offset + BAND][None, :, None] * back_pad[:, BAND - offset:BAND - offset + CLAT]
    return running

def interpolate(increment):
    padded = jnp.concatenate([increment[:, :, :1], increment, increment[:, :, -1:]], axis=2)
    even_rows = 0.75 * padded[:, :, 1:-1] + 0.25 * padded[:, :, :-2]
    odd_rows = 0.75 * padded[:, :, 1:-1] + 0.25 * padded[:, :, 2:]
    merid = jnp.stack([even_rows, odd_rows], axis=3).reshape(VARS, LEV, 2 * CLAT, NLON)
    shifted = jnp.roll(merid, -1, axis=3)
    return jnp.stack([merid, 0.5 * (merid + shifted)], axis=-1).reshape(VARS, LEV, 2 * CLAT, 2 * NLON)

def to_tiles(fine_field):
    shaped = fine_field.reshape(VARS, LEV, BANDS, 2 * CLAT_DEV, NTILE, TLON)
    return shaped.transpose(2, 4, 0, 1, 3, 5).reshape(-1)

def from_tiles(flat_tiles):
    shaped = flat_tiles.reshape(BANDS, NTILE, VARS, LEV, 2 * CLAT_DEV, TLON)
    return shaped.transpose(2, 3, 0, 4, 1, 5).reshape(VARS, LEV, 2 * CLAT, 2 * NLON)

def reference(members, alpha, zonal_loc, merid_coef, slot_tile, obs_count, obs_index, obs_value, obs_weight):
    band_ids = jnp.arange(BANDS, dtype=jnp.int32)[:, None, None]
    tile_ids = (band_ids * NTILE + slot_tile.astype(jnp.int32)) * TILE_CELLS
    global_points = (tile_ids[..., None] + obs_index.astype(jnp.int32)).reshape(-1)
    active = jnp.arange(OBS_TILE, dtype=jnp.int32)[None, None, None, :] < obs_count[..., None]
    current = alpha
    for iteration in range(ITERS):

        def add_member(running, member_pair):
            member_x, member_alpha = member_pair
            zonal_out = localize(member_alpha, merid_coef, zonal_loc)
            return (running + member_x.astype(jnp.float32) * zonal_out[None], None)
        increment, unused = lax.scan(add_member, jnp.zeros((VARS, LEV, CLAT, NLON), jnp.float32), (members, current))
        fine_field, pullback = jax.vjp(interpolate, increment)
        flat_tiles = to_tiles(fine_field)
        sampled = flat_tiles[global_points].reshape(obs_value.shape)
        residual = jnp.where(active, obs_weight * (sampled - obs_value), jnp.float32(0.0))
        fine_grad = jnp.zeros(flat_tiles.shape, jnp.float32).at[global_points].add(residual.reshape(-1))
        adjoint, = pullback(from_tiles(fine_grad))

        def member_grad(member_pair):
            member_x, member_alpha = member_pair
            weighted = lax.optimization_barrier(jnp.sum(member_x.astype(jnp.float32) * adjoint, axis=0)).astype(jnp.bfloat16)
            zonal_back = lax.dot_general(weighted.reshape(-1, NLON), zonal_loc, (((1,), (1,)), ((), ())), preferred_element_type=jnp.float32)
            return member_alpha + meridional_back(zonal_back.reshape(member_alpha.shape), merid_coef)
        gradient = lax.map(member_grad, (members, current))
        current = current - step_size * gradient
    return current
```

```python
import functools

import jax
import jax.numpy as jnp
import numpy as np
from jax import lax
from jax.experimental import pallas as pl
from jax.experimental.pallas import tpu as pltpu
from jax.sharding import PartitionSpec as P

TLON = 128
ITERS = 2
LANES = 128
OBS_CHUNK = 1024


step_size = 0.3


def band_exchange(to_prev, to_next):
    count = lax.axis_size("lat")
    even = lax.axis_index("lat") % 2 == 0
    first = [(i, i ^ 1) for i in range(count) if i ^ 1 < count]
    second = [(i, ((i + 1) ^ 1) - 1) for i in range(count) if 0 <= ((i + 1) ^ 1) - 1 < count]
    if to_prev is to_next:
        send_first = send_second = to_prev
    else:
        send_first = jnp.where(even, to_next, to_prev)
        send_second = jnp.where(even, to_prev, to_next)
    got_first = lax.ppermute(send_first, "lat", first)
    got_second = lax.ppermute(send_second, "lat", second)
    return jnp.where(even, got_second, got_first), jnp.where(even, got_first, got_second)


def core_swap(cells):
    count = lax.axis_size("mem")
    return lax.ppermute(cells, "mem", [(i, i ^ 1) for i in range(count)])


def chip_steps():
    count = lax.axis_size("mem")
    bits = [1 << b for b in range(1, count.bit_length() - 1)]
    return [
        [(i, i ^ bits[(step + i % 2) % len(bits)]) for i in range(count)]
        for step in range(len(bits))
    ]


def core_split(cells):
    core = lax.axis_index("mem") % 2
    half = cells.shape[0] // 2
    mine = lax.dynamic_slice_in_dim(cells, core * half, half, 0)
    other = lax.dynamic_slice_in_dim(cells, (1 - core) * half, half, 0)
    return mine, other


def member_sum(cells):
    mine, other = core_split(cells)
    total = mine + core_swap(other)
    for perm in chip_steps():
        total = total + lax.ppermute(total, "mem", perm)
    return total


def both_halves(mine):
    core = lax.axis_index("mem") % 2
    other = core_swap(mine)
    return jnp.concatenate(
        [jnp.where(core == 0, mine, other), jnp.where(core == 0, other, mine)], axis=0
    )


def split_two(x):
    top = x.astype(jnp.bfloat16)
    return top, (x - top.astype(jnp.float32)).astype(jnp.bfloat16)


def tile_kernel(tile_ref, count_ref, row_ref, lane_ref, index_ref, value_ref, weight_ref, out_ref):
    slot = pl.program_id(0)
    count = count_ref[slot]
    half = TLON // 2
    wide = half + 8
    rows = row_ref.shape[0]
    out_ref[...] = jnp.zeros_like(out_ref)
    spots = row_ref[...]
    lanes = lane_ref[...]
    coarse = 2 * lax.broadcasted_iota(jnp.int32, (wide, 1), 0)
    chunk = min(OBS_CHUNK, index_ref.shape[-1])

    def step(part, carry):
        @pl.when(part * chunk < count)
        def _():
            here = pl.ds(pl.multiple_of(part * chunk, chunk), chunk)
            index = index_ref[0, :, here]
            weight = weight_ref[0, :, here]
            place = lax.broadcasted_iota(jnp.int32, (1, chunk), 1) + part * chunk
            weight = jnp.where(place < count, weight, 0.0)
            pull = weight * value_ref[0, :, here]
            high = lax.shift_right_logical(index, TLON.bit_length() - 1)
            low = lax.bitwise_and(index, TLON - 1)
            at_row = jnp.where(spots == high, 1.0, 0.0).astype(jnp.bfloat16)
            contract = (((1,), (1,)), ((), ()))
            total = jnp.zeros((rows, TLON), jnp.float32)
            for piece in split_two(weight):
                at_lane = jnp.where(lanes == low, piece.astype(jnp.float32), 0.0)
                total += lax.dot_general(
                    at_row, at_lane.astype(jnp.bfloat16), contract, preferred_element_type=jnp.float32
                )
            apart = jnp.abs(low - coarse)
            share = jnp.where(apart == 0, 1.0, jnp.where(apart == 1, 0.5, 0.0))
            pulled = jnp.zeros((rows, wide), jnp.float32)
            for piece in split_two(pull):
                at_coarse = share * piece.astype(jnp.float32)
                pulled += lax.dot_general(
                    at_row, at_coarse.astype(jnp.bfloat16), contract, preferred_element_type=jnp.float32
                )
            pulled = jnp.concatenate(
                [pulled, jnp.zeros((rows, TLON - wide), jnp.float32)], axis=1
            )
            groups = out_ref.shape[1]
            step_rows = rows // groups
            for group in range(groups):
                mine = slice(group * step_rows, (group + 1) * step_rows)
                out_ref[0, group, :step_rows] += total[mine]
                out_ref[0, group, step_rows:] += pulled[mine]

        return carry

    lax.fori_loop(0, index_ref.shape[-1] // chunk, step, 0)
    step_rows = rows // out_ref.shape[1]
    marker = jnp.where(count > 0, tile_ref[slot] + 1, 0).astype(jnp.float32)
    lane = lax.broadcasted_iota(jnp.int32, (8, TLON), 1)
    for group in range(out_ref.shape[1]):
        block = out_ref[0, group, step_rows : step_rows + 8]
        out_ref[0, group, step_rows : step_rows + 8] = jnp.where(lane == TLON - 1, marker, block)


def tile_sums(tiles, counts, index, value, weight, var_count, lev_count, row_count):
    slots, length = index.shape
    var, par, lev, row = np.meshgrid(
        np.arange(var_count), np.arange(2), np.arange(lev_count), np.arange(row_count), indexing="ij"
    )
    spot = ((var * lev_count + lev) * row_count + row) * 2 + par
    spot = spot.reshape(-1, 1).astype(np.int32)
    lanes = np.arange(TLON).reshape(2, TLON // 2)
    lanes = (2 * (lanes % (TLON // 2)) + lanes // (TLON // 2)).reshape(-1, 1).astype(np.int32)
    rows = spot.shape[0]
    whole = lambda shape: pl.BlockSpec(shape, lambda s, *_: (0,) * len(shape))
    line = pl.BlockSpec((1, 1, length), lambda s, *_: (s, 0, 0))
    out = (slots, var_count, 2 * rows // var_count, TLON)
    return pl.pallas_call(
        tile_kernel,
        grid_spec=pltpu.PrefetchScalarGridSpec(
            num_scalar_prefetch=2,
            grid=(slots,),
            in_specs=[whole(spot.shape), whole(lanes.shape), line, line, line],
            out_specs=pl.BlockSpec((1,) + out[1:], lambda s, *_: (s, 0, 0, 0)),
        ),
        out_shape=jax.ShapeDtypeStruct(out, jnp.float32),
        compiler_params=pltpu.CompilerParams(vmem_limit_bytes=32 * 2**20),
        cost_estimate=pl.CostEstimate(
            flops=2 * slots * length * rows * 400, bytes_accessed=slots * rows * 1024, transcendentals=0
        ),
    )(
        tiles,
        counts,
        jnp.asarray(spot),
        jnp.asarray(lanes),
        index[:, None],
        value[:, None],
        weight[:, None],
    )


def field_kernel(mark_ref, slots_ref, weight_ref, pull_ref, where_ref):
    tile_count = where_ref.shape[0]
    half = TLON // 2

    def note(slot, carry):
        mark = mark_ref[slot]

        @pl.when(mark > 0)
        def _():
            where_ref[mark - 1] = slot

        return carry

    for tile in range(tile_count):
        where_ref[tile] = 0
    lax.fori_loop(0, mark_ref.shape[0], note, 0)
    rows = weight_ref.shape[1]
    lane = lax.broadcasted_iota(jnp.int32, (rows, TLON), 1)
    for pair in range(tile_count // 2):
        left = where_ref[2 * pair]
        right = where_ref[2 * pair + 1]
        before = where_ref[(2 * pair - 1) % tile_count]
        here = slice(pair * TLON, (pair + 1) * TLON)
        first, second = slots_ref[left, :rows], slots_ref[right, :rows]
        weight_ref[0, :, here] = jnp.where(lane < half, first, pltpu.roll(second, half, 1))
        weight_ref[1, :, here] = jnp.where(lane < half, pltpu.roll(first, half, 1), second)
        first, second = slots_ref[left, rows:], slots_ref[right, rows:]
        third = slots_ref[before, rows:]
        pull_ref[:, here] = (
            jnp.where(lane <= half, first, 0.0)
            + jnp.where(lane >= half, pltpu.roll(second, half, 1), 0.0)
            + jnp.where(lane == 0, pltpu.roll(third, half, 1), 0.0)
        )


def band_fields(slots, lon_cells):
    rows = slots.shape[1] // 2
    marks = slots[:, rows, TLON - 1].astype(jnp.int32)
    vmem = pl.BlockSpec(memory_space=pltpu.VMEM)
    return pl.pallas_call(
        field_kernel,
        in_specs=[pl.BlockSpec(memory_space=pltpu.SMEM), vmem],
        out_specs=[vmem, vmem],
        out_shape=[
            jax.ShapeDtypeStruct((2, rows, lon_cells), jnp.float32),
            jax.ShapeDtypeStruct((rows, lon_cells), jnp.float32),
        ],
        scratch_shapes=[pltpu.SMEM((2 * lon_cells // TLON,), jnp.int32)],
        compiler_params=pltpu.CompilerParams(vmem_limit_bytes=32 * 2**20),
        cost_estimate=pl.CostEstimate(
            flops=rows * lon_cells * 8, bytes_accessed=rows * lon_cells * 24, transcendentals=0
        ),
    )(marks, slots)


def observation_fields(tiles, counts, index, value, weight, var_count, lev_count, row_count, lon_cells):
    slots = tile_sums(tiles, counts, index, value, weight, var_count, lev_count, row_count)
    core = lax.axis_index("mem") % 2
    by_var = slots.transpose(1, 0, 2, 3)
    mine, other = core_split(by_var)
    held = jnp.concatenate([mine[0], core_swap(other)[0]], axis=0)
    for perm in chip_steps():
        held = jnp.concatenate([held, lax.ppermute(held, "mem", perm)], axis=0)
    return band_fields(held, lon_cells)


def pull_columns(weights, cells):
    odd = weights[1] * (0.5 * (cells + jnp.roll(cells, -1, axis=-1)))
    return weights[0] * cells + 0.5 * (odd + jnp.roll(odd, 1, axis=-1))


def observed_adjoint(inc, below, above, fields, rims, band_index, band_count):
    weights, pulls = fields
    south = band_index == 0
    north = band_index == band_count - 1
    first, last = inc[:, 0], inc[:, -1]
    lower = jnp.where(south, first, below)
    upper = jnp.where(north, last, above)
    down = jnp.concatenate([lower[:, None], inc[:, :-1]], axis=1)
    up = jnp.concatenate([inc[:, 1:], upper[:, None]], axis=1)
    even = pull_columns(weights[:, 0], 0.75 * inc + 0.25 * down) - pulls[0]
    odd = pull_columns(weights[:, 1], 0.75 * inc + 0.25 * up) - pulls[1]
    (rim_weight_below, rim_pull_below), (rim_weight_above, rim_pull_above) = rims
    odd_below = pull_columns(rim_weight_below, 0.75 * below + 0.25 * first) - rim_pull_below
    even_above = pull_columns(rim_weight_above, 0.75 * above + 0.25 * last) - rim_pull_above
    odd_below = jnp.where(south, even[:, 0], odd_below)
    even_above = jnp.where(north, odd[:, -1], even_above)
    odd_down = jnp.concatenate([odd_below[:, None], odd[:, :-1]], axis=1)
    even_up = jnp.concatenate([even[:, 1:], even_above[:, None]], axis=1)
    return 0.75 * (even + odd) + 0.25 * (odd_down + even_up)


def forward_rows(cells, coeffs, row_count, half_band):
    running = jnp.zeros(cells.shape[:2] + (row_count, cells.shape[3]), jnp.float32)
    for offset in range(2 * half_band + 1):
        running = running + coeffs[:, offset][None, None, :, None] * cells[:, :, offset : offset + row_count]
    return running


def backward_rows(cells, coeffs, row_count, half_band):
    running = jnp.zeros(cells.shape[:2] + (row_count, cells.shape[3]), jnp.float32)
    for offset in range(2 * half_band + 1):
        at = 2 * half_band - offset
        running = (
            running
            + coeffs[at : at + row_count, offset][None, None, :, None] * cells[:, :, at : at + row_count]
        )
    return running


def partial_increment(ext, coeffs, zonal_loc, members, half_band):
    spread = forward_rows(ext, coeffs, members.shape[3], half_band).astype(jnp.bfloat16)
    localized = jnp.dot(
        spread.reshape(-1, spread.shape[-1]), zonal_loc, preferred_element_type=jnp.float32
    ).reshape(spread.shape)
    return jnp.sum(members * localized[:, None], axis=0)


def zonal_backward(members, adjoint, zonal_loc):
    weighted = jnp.sum(members * adjoint[None], axis=1).astype(jnp.bfloat16)
    return lax.dot_general(
        weighted.reshape(-1, weighted.shape[-1]),
        zonal_loc,
        (((1,), (1,)), ((), ())),
        preferred_element_type=jnp.float32,
    ).reshape(weighted.shape)


def body(
    members, alpha, zonal_loc, merid_coef, slot_tile, obs_count, obs_index, obs_value, obs_weight
):
    half_band = merid_coef.shape[1] // 2
    _, var_count, lev_count, rows, lon_cells = members.shape
    band_index = lax.axis_index("lat")
    band_count = lax.axis_size("lat")
    slot_count = slot_tile.shape[-1]

    below, above = band_exchange(alpha[:, :, :half_band], alpha[:, :, -half_band:])
    ext = jnp.concatenate([below, alpha, above], axis=2)
    sent, below = lax.optimization_barrier((members, below))
    members_below, members_above = band_exchange(sent, sent)

    weights, pulls = observation_fields(
        slot_tile.reshape(-1),
        obs_count.reshape(-1),
        obs_index.reshape(slot_count, -1),
        obs_value.reshape(slot_count, -1),
        obs_weight.reshape(slot_count, -1),
        var_count,
        lev_count,
        rows,
        lon_cells,
    )
    weights = weights.reshape(2, 2, lev_count, rows, lon_cells)
    pulls = pulls.reshape(2, lev_count, rows, lon_cells)
    rim_below, rim_above = band_exchange(
        jnp.concatenate([weights[:, 0, :, 0], pulls[None, 0, :, 0]]),
        jnp.concatenate([weights[:, 1, :, -1], pulls[None, 1, :, -1]]),
    )
    rims = (rim_below[:2], rim_below[2]), (rim_above[:2], rim_above[2])

    coef_wide = jnp.pad(merid_coef, ((rows, rows), (0, 0)))
    coef_wide = lax.dynamic_slice_in_dim(coef_wide, band_index * rows, 3 * rows, 0)
    own_coef = coef_wide[rows : 2 * rows]
    row_at = band_index * rows + jnp.arange(-half_band, rows + half_band)
    on_grid = ((row_at >= 0) & (row_at < band_count * rows))[None, None, :, None]

    for iteration in range(ITERS):
        partial_value = partial_increment(ext, own_coef, zonal_loc, members, half_band)
        inc = member_sum(partial_value)[0]
        low, high = band_exchange(inc[:, 0], inc[:, -1])
        adjoint = observed_adjoint(inc, low, high, (weights, pulls), rims, band_index, band_count)
        if iteration + 1 < ITERS:
            low, high = band_exchange(adjoint, adjoint)
            halo = rows
        else:
            low, high = band_exchange(adjoint[:, :half_band], adjoint[:, -half_band:])
            halo = half_band
        adjoint = both_halves(jnp.concatenate([low, adjoint, high], axis=1)[None])
        wide_members = jnp.concatenate(
            [members_below[:, :, :, rows - halo :], members, members_above[:, :, :, :halo]], axis=3
        )
        zonal_back = zonal_backward(wide_members, adjoint, zonal_loc)
        coeffs = coef_wide[rows - halo : 2 * rows + halo]
        if iteration + 1 < ITERS:
            gradient = ext + backward_rows(zonal_back, coeffs, rows + 2 * half_band, half_band)
            ext = jnp.where(on_grid, ext - step_size * gradient, 0.0)
        else:
            current = ext[:, :, half_band:-half_band]
            gradient = current + backward_rows(zonal_back, coeffs, rows, half_band)
            current = current - step_size * gradient
    return current


def solution(mesh):
    in_specs = (
        P("mem", None, None, "lat", None),
        P("mem", None, "lat", None),
        P(),
        P(),
        P("lat", "mem", None),
        P("lat", "mem", None),
        P("lat", "mem", None, None),
        P("lat", "mem", None, None),
        P("lat", "mem", None, None),
    )
    out_specs = P("mem", None, "lat", None)
    return jax.shard_map(body, mesh=mesh, in_specs=in_specs, out_specs=out_specs, check_vma=False)
```

```python
import functools

import jax
import jax.numpy as jnp
import numpy as np
from jax import lax
from jax.experimental import pallas as pl
from jax.experimental.pallas import tpu as pltpu
from jax.sharding import PartitionSpec as P

TLON = 128
ITERS = 2
LANES = 128
OBS_CHUNK = 1024
PART_EVENTS = ("forward", "chip0", "chip1", "adjoint", None)
PARTS = len(PART_EVENTS)
EVEN, CORE, HAS_FIRST, HAS_SECOND, HAS_BELOW, HAS_ABOVE = range(6)


step_size = 0.3


def band_pairs(second):
    bands, groups = lax.axis_size("lat"), lax.axis_size("mem")
    perm = []
    for group in range(groups):
        for band in range(bands):
            other = ((band + second) ^ 1) - second
            if 0 <= other < bands:
                target = group * bands + other
            else:
                target = (group ^ 1) * bands + band
            perm.append((group * bands + band, target))
    return perm


def band_swap(send_first, send_second):
    axes = ("mem", "lat")
    return (
        lax.ppermute(send_first, axes, band_pairs(0)),
        lax.ppermute(send_second, axes, band_pairs(1)),
    )


def band_sides():
    band = lax.axis_index("lat")
    return band % 2 == 0, band > 0, band < lax.axis_size("lat") - 1


def by_partner(to_prev, to_next):
    even, _, _ = band_sides()
    return jnp.where(even, to_next, to_prev), jnp.where(even, to_prev, to_next)


def core_swap(cells):
    count = lax.axis_size("mem")
    return lax.ppermute(cells, "mem", [(i, i ^ 1) for i in range(count)])


def chip_steps():
    count = lax.axis_size("mem")
    bits = [1 << b for b in range(1, count.bit_length() - 1)]
    return [
        [(i, i ^ bits[(step + i % 2) % len(bits)]) for i in range(count)]
        for step in range(len(bits))
    ]


def core_split(cells):
    core = lax.axis_index("mem") % 2
    half = cells.shape[0] // 2
    mine = lax.dynamic_slice_in_dim(cells, core * half, half, 0)
    other = lax.dynamic_slice_in_dim(cells, (1 - core) * half, half, 0)
    return mine, other


def split_two(x):
    top = x.astype(jnp.bfloat16)
    return top, (x - top.astype(jnp.float32)).astype(jnp.bfloat16)


def tile_kernel(tile_ref, count_ref, row_ref, lane_ref, index_ref, value_ref, weight_ref, out_ref):
    slot = pl.program_id(0)
    count = count_ref[slot]
    half = TLON // 2
    wide = half + 8
    rows = row_ref.shape[0]
    out_ref[...] = jnp.zeros_like(out_ref)
    spots = row_ref[...]
    lanes = lane_ref[...]
    coarse = 2 * lax.broadcasted_iota(jnp.int32, (wide, 1), 0)
    chunk = min(OBS_CHUNK, index_ref.shape[-1])

    def step(part, carry):
        @pl.when(part * chunk < count)
        def _():
            here = pl.ds(pl.multiple_of(part * chunk, chunk), chunk)
            index = index_ref[0, :, here]
            weight = weight_ref[0, :, here]
            place = lax.broadcasted_iota(jnp.int32, (1, chunk), 1) + part * chunk
            weight = jnp.where(place < count, weight, 0.0)
            pull = weight * value_ref[0, :, here]
            high = lax.shift_right_logical(index, TLON.bit_length() - 1)
            low = lax.bitwise_and(index, TLON - 1)
            at_row = jnp.where(spots == high, 1.0, 0.0).astype(jnp.bfloat16)
            contract = (((1,), (1,)), ((), ()))
            total = jnp.zeros((rows, TLON), jnp.float32)
            for piece in split_two(weight):
                at_lane = jnp.where(lanes == low, piece.astype(jnp.float32), 0.0)
                total += lax.dot_general(
                    at_row, at_lane.astype(jnp.bfloat16), contract, preferred_element_type=jnp.float32
                )
            apart = jnp.abs(low - coarse)
            share = jnp.where(apart == 0, 1.0, jnp.where(apart == 1, 0.5, 0.0))
            pulled = jnp.zeros((rows, wide), jnp.float32)
            for piece in split_two(pull):
                at_coarse = share * piece.astype(jnp.float32)
                pulled += lax.dot_general(
                    at_row, at_coarse.astype(jnp.bfloat16), contract, preferred_element_type=jnp.float32
                )
            pulled = jnp.concatenate(
                [pulled, jnp.zeros((rows, TLON - wide), jnp.float32)], axis=1
            )
            groups = out_ref.shape[1]
            step_rows = rows // groups
            for group in range(groups):
                mine = slice(group * step_rows, (group + 1) * step_rows)
                out_ref[0, group, :step_rows] += total[mine]
                out_ref[0, group, step_rows:] += pulled[mine]

        return carry

    lax.fori_loop(0, index_ref.shape[-1] // chunk, step, 0)
    step_rows = rows // out_ref.shape[1]
    marker = jnp.where(count > 0, tile_ref[slot] + 1, 0).astype(jnp.float32)
    lane = lax.broadcasted_iota(jnp.int32, (8, TLON), 1)
    for group in range(out_ref.shape[1]):
        block = out_ref[0, group, step_rows : step_rows + 8]
        out_ref[0, group, step_rows : step_rows + 8] = jnp.where(lane == TLON - 1, marker, block)


def tile_sums(tiles, counts, index, value, weight, var_count, lev_count, row_count):
    slots, length = index.shape
    var, par, lev, row = np.meshgrid(
        np.arange(var_count), np.arange(2), np.arange(lev_count), np.arange(row_count), indexing="ij"
    )
    spot = ((var * lev_count + lev) * row_count + row) * 2 + par
    spot = spot.reshape(-1, 1).astype(np.int32)
    lanes = np.arange(TLON).reshape(2, TLON // 2)
    lanes = (2 * (lanes % (TLON // 2)) + lanes // (TLON // 2)).reshape(-1, 1).astype(np.int32)
    rows = spot.shape[0]
    whole = lambda shape: pl.BlockSpec(shape, lambda s, *_: (0,) * len(shape))
    line = pl.BlockSpec((1, 1, length), lambda s, *_: (s, 0, 0))
    out = (slots, var_count, 2 * rows // var_count, TLON)
    return pl.pallas_call(
        tile_kernel,
        grid_spec=pltpu.PrefetchScalarGridSpec(
            num_scalar_prefetch=2,
            grid=(slots,),
            in_specs=[whole(spot.shape), whole(lanes.shape), line, line, line],
            out_specs=pl.BlockSpec((1,) + out[1:], lambda s, *_: (s, 0, 0, 0)),
        ),
        out_shape=jax.ShapeDtypeStruct(out, jnp.float32),
        compiler_params=pltpu.CompilerParams(vmem_limit_bytes=32 * 2**20),
        cost_estimate=pl.CostEstimate(
            flops=2 * slots * length * rows * 400, bytes_accessed=slots * rows * 1024, transcendentals=0
        ),
    )(
        tiles,
        counts,
        jnp.asarray(spot),
        jnp.asarray(lanes),
        index[:, None],
        value[:, None],
        weight[:, None],
    )


def field_kernel(mark_ref, slots_ref, weight_ref, pull_ref, where_ref):
    tile_count = where_ref.shape[0]
    half = TLON // 2

    def note(slot, carry):
        mark = mark_ref[slot]

        @pl.when(mark > 0)
        def _():
            where_ref[mark - 1] = slot

        return carry

    for tile in range(tile_count):
        where_ref[tile] = 0
    lax.fori_loop(0, mark_ref.shape[0], note, 0)
    rows = weight_ref.shape[1]
    lane = lax.broadcasted_iota(jnp.int32, (rows, TLON), 1)
    for pair in range(tile_count // 2):
        left = where_ref[2 * pair]
        right = where_ref[2 * pair + 1]
        before = where_ref[(2 * pair - 1) % tile_count]
        here = slice(pair * TLON, (pair + 1) * TLON)
        first, second = slots_ref[left, :rows], slots_ref[right, :rows]
        weight_ref[0, :, here] = jnp.where(lane < half, first, pltpu.roll(second, half, 1))
        weight_ref[1, :, here] = jnp.where(lane < half, pltpu.roll(first, half, 1), second)
        first, second = slots_ref[left, rows:], slots_ref[right, rows:]
        third = slots_ref[before, rows:]
        pull_ref[:, here] = (
            jnp.where(lane <= half, first, 0.0)
            + jnp.where(lane >= half, pltpu.roll(second, half, 1), 0.0)
            + jnp.where(lane == 0, pltpu.roll(third, half, 1), 0.0)
        )


def band_fields(slots, lon_cells):
    rows = slots.shape[1] // 2
    marks = slots[:, rows, TLON - 1].astype(jnp.int32)
    vmem = pl.BlockSpec(memory_space=pltpu.VMEM)
    return pl.pallas_call(
        field_kernel,
        in_specs=[pl.BlockSpec(memory_space=pltpu.SMEM), vmem],
        out_specs=[vmem, vmem],
        out_shape=[
            jax.ShapeDtypeStruct((2, rows, lon_cells), jnp.float32),
            jax.ShapeDtypeStruct((rows, lon_cells), jnp.float32),
        ],
        scratch_shapes=[pltpu.SMEM((2 * lon_cells // TLON,), jnp.int32)],
        compiler_params=pltpu.CompilerParams(vmem_limit_bytes=32 * 2**20),
        cost_estimate=pl.CostEstimate(
            flops=rows * lon_cells * 8, bytes_accessed=rows * lon_cells * 24, transcendentals=0
        ),
    )(marks, slots)


def observation_slots(tiles, counts, index, value, weight, var_count, lev_count, row_count):
    slots = tile_sums(tiles, counts, index, value, weight, var_count, lev_count, row_count)
    mine, other = core_split(slots.transpose(1, 0, 2, 3))
    return jnp.concatenate([mine[0], core_swap(other)[0]], axis=0)


def pull_columns(weight, odd_weight, cells):
    lon = cells.shape[-1]
    odd = odd_weight * (0.5 * (cells + pltpu.roll(cells, lon - 1, cells.ndim - 1)))
    return weight * cells + 0.5 * (odd + pltpu.roll(odd, 1, cells.ndim - 1))


def observe_kernel(
    flag_ref, inc_ref, first_ref, second_ref, weight_ref, pull_ref, rim_first_ref, rim_second_ref, out_ref
):
    even = flag_ref[EVEN] == 1
    has_below, has_above = flag_ref[HAS_BELOW] == 1, flag_ref[HAS_ABOVE] == 1
    levels, rows, lon = inc_ref.shape
    first, second = first_ref[...], second_ref[...]
    lowest = jnp.concatenate([inc_ref[lev, 0:1] for lev in range(levels)], axis=0)
    highest = jnp.concatenate([inc_ref[lev, rows - 1 : rows] for lev in range(levels)], axis=0)
    below = jnp.where(has_below, jnp.where(even, second, first), lowest)
    above = jnp.where(has_above, jnp.where(even, first, second), highest)
    rim_below = [jnp.where(even, rim_second_ref[i], rim_first_ref[i]) for i in range(3)]
    rim_above = [jnp.where(even, rim_first_ref[i], rim_second_ref[i]) for i in range(3)]
    odd_below = pull_columns(rim_below[0], rim_below[1], 0.75 * below + 0.25 * lowest) - rim_below[2]
    even_above = pull_columns(rim_above[0], rim_above[1], 0.75 * above + 0.25 * highest) - rim_above[2]
    row = lax.broadcasted_iota(jnp.int32, (rows, lon), 0)
    for lev in range(levels):
        cells = inc_ref[lev]
        down = jnp.where(row == 0, below[lev : lev + 1], pltpu.roll(cells, 1, 0))
        up = jnp.where(row == rows - 1, above[lev : lev + 1], pltpu.roll(cells, rows - 1, 0))
        low = pull_columns(weight_ref[0, 0, lev], weight_ref[1, 0, lev], 0.75 * cells + 0.25 * down) - pull_ref[0, lev]
        high = pull_columns(weight_ref[0, 1, lev], weight_ref[1, 1, lev], 0.75 * cells + 0.25 * up) - pull_ref[1, lev]
        from_below = jnp.where(has_below, odd_below[lev : lev + 1], low[0:1])
        from_above = jnp.where(has_above, even_above[lev : lev + 1], high[rows - 1 : rows])
        high_down = jnp.where(row == 0, from_below, pltpu.roll(high, 1, 0))
        low_up = jnp.where(row == rows - 1, from_above, pltpu.roll(low, rows - 1, 0))
        out_ref[lev] = 0.75 * (low + high) + 0.25 * (high_down + low_up)


def row_groups(lines):
    starts = list(range(0, lines - 7, 8))
    return starts if starts[-1] + 8 == lines else starts + [lines - 8]


def strided(ref, chunk, start, rows):
    return ref[chunk, pl.ds(start, 8, stride=rows), :]


def to_chunks(ref, cells):
    for chunk in range(ref.shape[0]):
        ref[chunk] = cells[:, chunk * LANES : (chunk + 1) * LANES]


def spread_rows(cells, coef_ref, base, taps):
    out = []
    for row in range(len(cells) - taps + 1):
        total = coef_ref[base + row * taps] * cells[row]
        for tap in range(1, taps):
            total += coef_ref[base + row * taps + tap] * cells[row + tap]
        out.append(total)
    return out


def pull_rows(cells, coef_ref, base, taps):
    out = []
    for row in range(len(cells) - taps + 1):
        total = coef_ref[base + row * taps] * cells[row + taps - 1]
        for tap in range(1, taps):
            total += coef_ref[base + row * taps + tap] * cells[row + taps - 1 - tap]
        out.append(total)
    return out


def sum_members(spread_ref, zonal_ref, members_ref, inc_ref):
    size, variables, levels, rows, lon = members_ref.shape
    spread = jnp.concatenate(
        [spread_ref[chunk].astype(jnp.bfloat16) for chunk in range(spread_ref.shape[0])], axis=1
    )
    wide = LANES * 3 if lon % (LANES * 3) == 0 else LANES
    for start in range(0, lon, wide):
        lanes = slice(start, start + wide)
        localized = jnp.dot(spread, zonal_ref[:, lanes], preferred_element_type=jnp.float32)
        localized = localized.reshape(size, levels, rows, wide)
        for var in range(variables):
            total = members_ref[0, var, :, :, lanes].astype(jnp.float32) * localized[0]
            for k in range(1, size):
                total += members_ref[k, var, :, :, lanes].astype(jnp.float32) * localized[k]
            inc_ref[var, :, :, lanes] = total


def edge_kernel(alpha_ref, first_ref, second_ref):
    even = lax.rem(lax.axis_index("lat"), 2) == 0
    lines, rows = alpha_ref.shape[:2]
    half = first_ref.shape[0] // lines

    def step(pair, carry):
        one, two = alpha_ref[2 * pair], alpha_ref[2 * pair + 1]
        here = pl.ds(pl.multiple_of(pair * 2 * half, 8), 2 * half)
        head = jnp.concatenate([one[:half], two[:half]], axis=0)
        tail = jnp.concatenate([one[rows - half :], two[rows - half :]], axis=0)
        first_ref[here, :] = jnp.where(even, tail, head)
        second_ref[here, :] = jnp.where(even, head, tail)
        return carry

    lax.fori_loop(0, lines // 2, step, 0, unroll=2)


def forward_kernel(
    flag_ref,
    coef_ref,
    alpha_ref,
    first_ref,
    second_ref,
    zonal_ref,
    members_ref,
    inc_ref,
    own_ref,
    below_ref,
    above_ref,
    spread_ref,
):
    rows = members_ref.shape[3]
    half_band = first_ref.shape[0] * rows // alpha_ref.shape[0]
    taps = 2 * half_band + 1
    even = flag_ref[EVEN] == 1
    to_chunks(own_ref, alpha_ref[...])
    first = jnp.where(flag_ref[HAS_FIRST] == 1, first_ref[...], 0.0)
    second = jnp.where(flag_ref[HAS_SECOND] == 1, second_ref[...], 0.0)
    to_chunks(below_ref, jnp.where(even, second, first))
    to_chunks(above_ref, jnp.where(even, first, second))

    def step(chunk, carry):
        for start in row_groups(own_ref.shape[1] // rows):
            cells = wide_rows(own_ref, below_ref, above_ref, chunk, start, rows, half_band)
            for r, total in enumerate(spread_rows(cells, coef_ref, 0, taps)):
                spread_ref[chunk, pl.ds(start * rows + r, 8, stride=rows), :] = total
        return carry

    lax.fori_loop(0, own_ref.shape[0], step, 0)
    sum_members(spread_ref, zonal_ref, members_ref, inc_ref)


def wide_rows(own_ref, below_ref, above_ref, chunk, start, rows, half_band):
    below = [strided(below_ref, chunk, start * half_band + r, half_band) for r in range(half_band)]
    own = [strided(own_ref, chunk, start * rows + r, rows) for r in range(rows)]
    above = [strided(above_ref, chunk, start * half_band + r, half_band) for r in range(half_band)]
    return below + own + above


def zonal_back(flag_ref, adjoints, members, zonal_ref, weighted_ref, back_ref):
    lines = back_ref.shape[1] // 3
    even, core = flag_ref[EVEN], flag_ref[CORE]
    places = (lines, even * (2 * lines), (1 - even) * (2 * lines))
    there = (None, flag_ref[HAS_FIRST] == 1, flag_ref[HAS_SECOND] == 1)
    for number, (place, parts) in enumerate(zip(places, members)):
        mine_ref, other_ref = adjoints[2 * number : 2 * number + 2]
        done = 0
        for part_ref in parts:
            size, _, levels, rows, lon = part_ref.shape
            flat = levels * rows

            def step(
                k, carry, part_ref=part_ref, mine_ref=mine_ref, other_ref=other_ref, place=place, done=done, number=number
            ):
                total = part_ref[k, core].astype(jnp.float32) * mine_ref[...]
                total += part_ref[k, 1 - core].astype(jnp.float32) * other_ref[...]
                if there[number] is not None:
                    total = jnp.where(there[number], total, 0.0)
                at = pl.multiple_of(place + (k + done) * flat, 16)
                weighted_ref[pl.ds(at, flat), :] = total.reshape(flat, lon).astype(jnp.bfloat16)
                return carry

            lax.fori_loop(0, size, step, 0)
            done += size
    lon = zonal_ref.shape[0]
    wide = LANES * 3 if lon % (LANES * 3) == 0 else LANES
    for tile in range(3):
        here = slice(tile * lines, (tile + 1) * lines)
        weighted = weighted_ref[here, :]
        for start in range(0, lon, wide):
            back = lax.dot_general(
                weighted,
                zonal_ref[start : start + wide, :],
                (((1,), (1,)), ((), ())),
                preferred_element_type=jnp.float32,
            )
            for part in range(wide // LANES):
                back_ref[start // LANES + part, here, :] = back[:, part * LANES : (part + 1) * LANES]


def back_rows(back_ref, chunk, start, rows, halo):
    lines = back_ref.shape[1] // 3
    return [
        strided(back_ref, chunk, (at // rows) * lines + start * rows + at % rows, rows)
        for at in range(rows - halo, 2 * rows + halo)
    ]


def between_kernel(parts, *refs):
    flag_ref, coef_ref, own_ref, below_ref, above_ref, zonal_ref = refs[:6]
    adjoints = refs[6:12]
    members_ref = refs[12]
    partners = refs[13 : 13 + 2 * parts]
    inc_ref, current_ref, weighted_ref, back_ref, spread_ref = refs[13 + 2 * parts :]
    rows = members_ref.shape[3]
    lines = own_ref.shape[1]
    half_band = below_ref.shape[1] * rows // lines
    taps = 2 * half_band + 1
    zonal_back(
        flag_ref, adjoints, ((members_ref,), partners[:parts], partners[parts:]), zonal_ref, weighted_ref, back_ref
    )

    def step(chunk, carry):
        for start in row_groups(lines // rows):
            back = back_rows(back_ref, chunk, start, rows, 2 * half_band)
            pulled = pull_rows(back, coef_ref, rows * taps, taps)
            cells = wide_rows(own_ref, below_ref, above_ref, chunk, start, rows, half_band)
            cells = [c - step_size * (c + p) for c, p in zip(cells, pulled)]
            for r in range(rows):
                current_ref[chunk, pl.ds(start * rows + r, 8, stride=rows), :] = cells[half_band + r]
            for r, total in enumerate(spread_rows(cells, coef_ref, 0, taps)):
                spread_ref[chunk, pl.ds(start * rows + r, 8, stride=rows), :] = total
        return carry

    lax.fori_loop(0, own_ref.shape[0], step, 0)
    sum_members(spread_ref, zonal_ref, members_ref, inc_ref)


def last_kernel(parts, taps, *refs):
    flag_ref, coef_ref, own_ref, zonal_ref = refs[:4]
    adjoints = refs[4:10]
    members_ref = refs[10]
    partners = refs[11 : 11 + 2 * parts]
    out_ref, weighted_ref, back_ref, current_ref = refs[11 + 2 * parts :]
    rows = members_ref.shape[3]
    half_band = taps // 2
    zonal_back(
        flag_ref, adjoints, ((members_ref,), partners[:parts], partners[parts:]), zonal_ref, weighted_ref, back_ref
    )

    def step(chunk, carry):
        for start in row_groups(own_ref.shape[1] // rows):
            back = back_rows(back_ref, chunk, start, rows, half_band)
            for r, pulled in enumerate(pull_rows(back, coef_ref, (rows + half_band) * taps, taps)):
                here = pl.ds(start * rows + r, 8, stride=rows)
                cell = own_ref[chunk, here, :]
                current_ref[chunk, here, :] = cell - step_size * (cell + pulled)
        return carry

    lax.fori_loop(0, own_ref.shape[0], step, 0)
    for chunk in range(own_ref.shape[0]):
        out_ref[:, chunk * LANES : (chunk + 1) * LANES] = current_ref[chunk]


def call(kernel, operands, outs, scratch, flops):
    vmem = pl.BlockSpec(memory_space=pltpu.VMEM)
    moved = sum(int(np.prod(x.shape)) * x.dtype.itemsize for x in list(operands) + list(outs))
    return pl.pallas_call(
        kernel,
        in_specs=[pl.BlockSpec(memory_space=pltpu.SMEM)] + [vmem] * (len(operands) - 1),
        out_specs=[vmem] * len(outs),
        out_shape=list(outs),
        scratch_shapes=list(scratch),
        compiler_params=pltpu.CompilerParams(vmem_limit_bytes=28 * 2**20),
        cost_estimate=pl.CostEstimate(flops=flops, bytes_accessed=moved, transcendentals=0),
    )(*operands)


def coefficient_kernel(rows, coef_ref, out_ref):
    count, taps = coef_ref.shape
    half_band = taps // 2
    first = lax.axis_index("lat") * rows

    def write(place, row, tap, on_grid):
        value = jnp.where(on_grid, coef_ref[jnp.clip(row, 0, count - 1), tap], 0.0)
        out_ref[place] = jnp.full(out_ref.shape[1:], value, jnp.float32)

    def forward(row, carry):
        for tap in range(taps):
            write(row * taps + tap, first + row, tap, True)
        return carry

    def backward(row, carry):
        target = first + row - half_band
        for tap in range(taps):
            source = target + half_band - tap
            on_grid = (target >= 0) & (target < count) & (source >= 0) & (source < count)
            write((rows + row) * taps + tap, source, tap, on_grid)
        return carry

    lax.fori_loop(0, rows, forward, 0)
    lax.fori_loop(0, rows + 2 * half_band, backward, 0)


def stencil_coefficients(merid_coef, rows):
    taps = merid_coef.shape[1]
    shape = ((2 * rows + taps - 1) * taps, 8, LANES)
    return pl.pallas_call(
        functools.partial(coefficient_kernel, rows),
        in_specs=[pl.BlockSpec(memory_space=pltpu.SMEM)],
        out_specs=pl.BlockSpec(memory_space=pltpu.VMEM),
        out_shape=jax.ShapeDtypeStruct(shape, jnp.float32),
        cost_estimate=pl.CostEstimate(flops=0, bytes_accessed=shape[0] * 4096, transcendentals=0),
    )(merid_coef)


def band_setup(held, lev_count, rows, lon_cells):
    weights, pulls = band_fields(held, lon_cells)
    weights = weights.reshape(2, 2, lev_count, rows, lon_cells)
    pulls = pulls.reshape(2, lev_count, rows, lon_cells)
    rims = band_swap(
        *by_partner(
            jnp.concatenate([weights[:, 0, :, 0], pulls[None, 0, :, 0]]),
            jnp.concatenate([weights[:, 1, :, -1], pulls[None, 1, :, -1]]),
        )
    )
    return weights, pulls, rims


def body(
    members, alpha, zonal_loc, merid_coef, slot_tile, obs_count, obs_index, obs_value, obs_weight
):
    half_band = merid_coef.shape[1] // 2
    _, var_count, lev_count, rows, lon_cells = members.shape
    slot_count = slot_tile.shape[-1]

    members_per = members.shape[0]
    lines = members_per * lev_count * rows
    even, has_below, has_above = band_sides()
    first_there = jnp.where(even, has_above, has_below)
    second_there = jnp.where(even, has_below, has_above)
    core = lax.axis_index("mem") % 2
    flags = jnp.stack(
        [x.astype(jnp.int32) for x in (even, core, first_there, second_there, has_below, has_above)]
    )

    edge_lines = members_per * lev_count * half_band
    edge_shape = jax.ShapeDtypeStruct((edge_lines, lon_cells), jnp.float32)
    vmem = pl.BlockSpec(memory_space=pltpu.VMEM)
    sends = pl.pallas_call(
        edge_kernel,
        in_specs=[vmem],
        out_specs=[vmem, vmem],
        out_shape=[edge_shape, edge_shape],
        compiler_params=pltpu.CompilerParams(vmem_limit_bytes=16 * 2**20),
        cost_estimate=pl.CostEstimate(flops=0, bytes_accessed=16 * edge_lines * lon_cells, transcendentals=0),
    )(alpha.reshape(-1, rows, lon_cells))
    obs_index, obs_value, obs_weight, sends = lax.optimization_barrier((obs_index, obs_value, obs_weight, sends))
    halo_first, halo_second = band_swap(*sends)
    coeffs = stencil_coefficients(merid_coef, rows)
    own = alpha.reshape(lines, lon_cells)

    cuts = [0] + [members_per * (i + 1) // PARTS for i in range(PARTS)]
    parts = [members[x:y] for x, y in zip(cuts[:-1], cuts[1:])]

    held = observation_slots(
        slot_tile.reshape(-1),
        obs_count.reshape(-1),
        obs_index.reshape(slot_count, -1),
        obs_value.reshape(slot_count, -1),
        obs_weight.reshape(slot_count, -1),
        var_count,
        lev_count,
        rows,
    )
    steps = chip_steps()
    for number, perm in enumerate(steps):
        if number == len(steps) - 1:
            halo_first, halo_second, held = lax.optimization_barrier((halo_first, halo_second, held))
        held = jnp.concatenate([held, lax.ppermute(held, "mem", perm)], axis=0)
    fetched = [band_swap(part, part) for part in parts]

    def pin(value, event):
        for number, name in enumerate(PART_EVENTS):
            if name == event:
                value, fetched[number] = lax.optimization_barrier((value, fetched[number]))
        return value

    inc_shape = jax.ShapeDtypeStruct((var_count, lev_count, rows, lon_cells), jnp.float32)
    line_shape = jax.ShapeDtypeStruct((lines, lon_cells), jnp.float32)
    chunks = lon_cells // LANES
    chunk_shape = jax.ShapeDtypeStruct((chunks, lines, LANES), jnp.float32)
    halo_shape = jax.ShapeDtypeStruct((chunks, halo_first.shape[0], LANES), jnp.float32)
    zonal_flops = 2 * lines * lon_cells * lon_cells
    chunk_scratch = pltpu.VMEM((chunks, lines, LANES), jnp.float32)
    weighted_scratch = pltpu.VMEM((3 * lines, lon_cells), jnp.bfloat16)
    back_scratch = pltpu.VMEM((chunks, 3 * lines, LANES), jnp.float32)
    partial_value, own, below, above = call(
        forward_kernel,
        (flags, coeffs, own, halo_first, halo_second, zonal_loc, members),
        [inc_shape, chunk_shape, halo_shape, halo_shape],
        [chunk_scratch],
        zonal_flops,
    )
    partial_value = pin(partial_value, "forward")
    for iteration in range(ITERS):
        mine, other = core_split(partial_value)
        inc = mine + core_swap(other)
        if iteration == 0:
            inc, held = lax.optimization_barrier((inc, held))
            weights, pulls, rims = band_setup(held, lev_count, rows, lon_cells)
        for number, perm in enumerate(steps):
            inc = inc + lax.ppermute(inc, "mem", perm)
            if iteration == 0 and number == len(steps) - 1:
                inc, rims = lax.optimization_barrier((inc, rims))
            if iteration == 0:
                inc = pin(inc, f"chip{number}")
        inc = inc[0]
        edges = band_swap(*by_partner(inc[:, 0], inc[:, -1]))
        (adjoint,) = call(
            observe_kernel,
            (flags, inc, *edges, weights, pulls, *rims),
            [jax.ShapeDtypeStruct(inc.shape, jnp.float32)],
            [],
            40 * 2 * inc.size,
        )
        if iteration == 0:
            adjoint = pin(adjoint, "adjoint")
        first, second = band_swap(adjoint, adjoint)
        halves = []
        for cells in (adjoint, first, second):
            halves += [cells, core_swap(cells)]
        partners = [x[0] for x in fetched] + [x[1] for x in fetched]
        if iteration + 1 < ITERS:
            partial_value, own = call(
                functools.partial(between_kernel, PARTS),
                (flags, coeffs, own, below, above, zonal_loc, *halves, members, *partners),
                [inc_shape, chunk_shape],
                [weighted_scratch, back_scratch, chunk_scratch],
                4 * zonal_flops,
            )
        else:
            (own,) = call(
                functools.partial(last_kernel, PARTS, 2 * half_band + 1),
                (flags, coeffs, own, zonal_loc, *halves, members, *partners),
                [line_shape],
                [weighted_scratch, back_scratch, chunk_scratch],
                3 * zonal_flops,
            )
    return own.reshape(alpha.shape)


def solution(mesh):
    in_specs = (
        P("mem", None, None, "lat", None),
        P("mem", None, "lat", None),
        P(),
        P(),
        P("lat", "mem", None),
        P("lat", "mem", None),
        P("lat", "mem", None, None),
        P("lat", "mem", None, None),
        P("lat", "mem", None, None),
    )
    out_specs = P("mem", None, "lat", None)
    return jax.shard_map(body, mesh=mesh, in_specs=in_specs, out_specs=out_specs, check_vma=False)
```

```python
import functools

import jax
import jax.numpy as jnp
import numpy as np
from jax import lax
from jax.experimental import pallas as pl
from jax.experimental.pallas import tpu as pltpu
from jax.sharding import PartitionSpec as P

TLON = 128
ITERS = 2
LANES = 128
OBS_CHUNK = 1024
PARTS = ((2, "forward"), (3, "chip0"), (3, "chip1"), (1, "adjoint"), (1, None))
EVEN, CORE, HAS_FIRST, HAS_SECOND, HAS_BELOW, HAS_ABOVE = range(6)


step_size = 0.3


def band_pairs(second):
    bands, groups = lax.axis_size("lat"), lax.axis_size("mem")
    perm = []
    for group in range(groups):
        for band in range(bands):
            other = ((band + second) ^ 1) - second
            if 0 <= other < bands:
                target = group * bands + other
            else:
                target = (group ^ 1) * bands + band
            perm.append((group * bands + band, target))
    return perm


def band_swap(send_first, send_second):
    axes = ("mem", "lat")
    return (
        lax.ppermute(send_first, axes, band_pairs(0)),
        lax.ppermute(send_second, axes, band_pairs(1)),
    )


def band_sides():
    band = lax.axis_index("lat")
    return band % 2 == 0, band > 0, band < lax.axis_size("lat") - 1


def by_partner(to_prev, to_next):
    even, _, _ = band_sides()
    return jnp.where(even, to_next, to_prev), jnp.where(even, to_prev, to_next)


def core_swap(cells):
    count = lax.axis_size("mem")
    return lax.ppermute(cells, "mem", [(i, i ^ 1) for i in range(count)])


def chip_steps():
    count = lax.axis_size("mem")
    bits = [1 << b for b in range(1, count.bit_length() - 1)]
    return [
        [(i, i ^ bits[(step + i % 2) % len(bits)]) for i in range(count)]
        for step in range(len(bits))
    ]


def core_split(cells):
    core = lax.axis_index("mem") % 2
    half = cells.shape[0] // 2
    mine = lax.dynamic_slice_in_dim(cells, core * half, half, 0)
    other = lax.dynamic_slice_in_dim(cells, (1 - core) * half, half, 0)
    return mine, other


def split_two(x):
    top = x.astype(jnp.bfloat16)
    return top, (x - top.astype(jnp.float32)).astype(jnp.bfloat16)


def tile_kernel(tile_ref, count_ref, row_ref, lane_ref, index_ref, value_ref, weight_ref, out_ref):
    slot = pl.program_id(0)
    count = count_ref[slot]
    half = TLON // 2
    wide = half + 8
    rows = row_ref.shape[0]
    out_ref[...] = jnp.zeros_like(out_ref)
    spots = row_ref[...]
    lanes = lane_ref[...]
    coarse = 2 * lax.broadcasted_iota(jnp.int32, (wide, 1), 0)
    chunk = min(OBS_CHUNK, index_ref.shape[-1])

    def step(part, carry):
        @pl.when(part * chunk < count)
        def _():
            here = pl.ds(pl.multiple_of(part * chunk, chunk), chunk)
            index = index_ref[0, :, here]
            weight = weight_ref[0, :, here]
            place = lax.broadcasted_iota(jnp.int32, (1, chunk), 1) + part * chunk
            weight = jnp.where(place < count, weight, 0.0)
            pull = weight * value_ref[0, :, here]
            high = lax.shift_right_logical(index, TLON.bit_length() - 1)
            low = lax.bitwise_and(index, TLON - 1)
            at_row = jnp.where(spots == high, 1.0, 0.0).astype(jnp.bfloat16)
            contract = (((1,), (1,)), ((), ()))
            total = jnp.zeros((rows, TLON), jnp.float32)
            for piece in split_two(weight):
                at_lane = jnp.where(lanes == low, piece.astype(jnp.float32), 0.0)
                total += lax.dot_general(
                    at_row, at_lane.astype(jnp.bfloat16), contract, preferred_element_type=jnp.float32
                )
            apart = jnp.abs(low - coarse)
            share = jnp.where(apart == 0, 1.0, jnp.where(apart == 1, 0.5, 0.0))
            pulled = jnp.zeros((rows, wide), jnp.float32)
            for piece in split_two(pull):
                at_coarse = share * piece.astype(jnp.float32)
                pulled += lax.dot_general(
                    at_row, at_coarse.astype(jnp.bfloat16), contract, preferred_element_type=jnp.float32
                )
            pulled = jnp.concatenate(
                [pulled, jnp.zeros((rows, TLON - wide), jnp.float32)], axis=1
            )
            groups = out_ref.shape[1]
            step_rows = rows // groups
            for group in range(groups):
                mine = slice(group * step_rows, (group + 1) * step_rows)
                out_ref[0, group, :step_rows] += total[mine]
                out_ref[0, group, step_rows:] += pulled[mine]

        return carry

    lax.fori_loop(0, index_ref.shape[-1] // chunk, step, 0)
    step_rows = rows // out_ref.shape[1]
    marker = jnp.where(count > 0, tile_ref[slot] + 1, 0).astype(jnp.float32)
    lane = lax.broadcasted_iota(jnp.int32, (8, TLON), 1)
    for group in range(out_ref.shape[1]):
        block = out_ref[0, group, step_rows : step_rows + 8]
        out_ref[0, group, step_rows : step_rows + 8] = jnp.where(lane == TLON - 1, marker, block)


def tile_sums(tiles, counts, index, value, weight, var_count, lev_count, row_count):
    slots, length = index.shape
    var, par, lev, row = np.meshgrid(
        np.arange(var_count), np.arange(2), np.arange(lev_count), np.arange(row_count), indexing="ij"
    )
    spot = ((var * lev_count + lev) * row_count + row) * 2 + par
    spot = spot.reshape(-1, 1).astype(np.int32)
    lanes = np.arange(TLON).reshape(2, TLON // 2)
    lanes = (2 * (lanes % (TLON // 2)) + lanes // (TLON // 2)).reshape(-1, 1).astype(np.int32)
    rows = spot.shape[0]
    whole = lambda shape: pl.BlockSpec(shape, lambda s, *_: (0,) * len(shape))
    line = pl.BlockSpec((1, 1, length), lambda s, *_: (s, 0, 0))
    out = (slots, var_count, 2 * rows // var_count, TLON)
    return pl.pallas_call(
        tile_kernel,
        grid_spec=pltpu.PrefetchScalarGridSpec(
            num_scalar_prefetch=2,
            grid=(slots,),
            in_specs=[whole(spot.shape), whole(lanes.shape), line, line, line],
            out_specs=pl.BlockSpec((1,) + out[1:], lambda s, *_: (s, 0, 0, 0)),
        ),
        out_shape=jax.ShapeDtypeStruct(out, jnp.float32),
        compiler_params=pltpu.CompilerParams(vmem_limit_bytes=16 * 2**20),
        cost_estimate=pl.CostEstimate(
            flops=2 * slots * length * rows * 400, bytes_accessed=slots * rows * 1024, transcendentals=0
        ),
    )(
        tiles,
        counts,
        jnp.asarray(spot),
        jnp.asarray(lanes),
        index[:, None],
        value[:, None],
        weight[:, None],
    )


def field_kernel(mark_ref, slots_ref, weight_ref, pull_ref, where_ref):
    tile_count = where_ref.shape[0]
    half = TLON // 2

    def note(slot, carry):
        mark = mark_ref[slot]

        @pl.when(mark > 0)
        def _():
            where_ref[mark - 1] = slot

        return carry

    for tile in range(tile_count):
        where_ref[tile] = 0
    lax.fori_loop(0, mark_ref.shape[0], note, 0)
    rows = weight_ref.shape[1]
    lane = lax.broadcasted_iota(jnp.int32, (rows, TLON), 1)
    for pair in range(tile_count // 2):
        left = where_ref[2 * pair]
        right = where_ref[2 * pair + 1]
        before = where_ref[(2 * pair - 1) % tile_count]
        here = slice(pair * TLON, (pair + 1) * TLON)
        first, second = slots_ref[left, :rows], slots_ref[right, :rows]
        weight_ref[0, :, here] = jnp.where(lane < half, first, pltpu.roll(second, half, 1))
        weight_ref[1, :, here] = jnp.where(lane < half, pltpu.roll(first, half, 1), second)
        first, second = slots_ref[left, rows:], slots_ref[right, rows:]
        third = slots_ref[before, rows:]
        pull_ref[:, here] = (
            jnp.where(lane <= half, first, 0.0)
            + jnp.where(lane >= half, pltpu.roll(second, half, 1), 0.0)
            + jnp.where(lane == 0, pltpu.roll(third, half, 1), 0.0)
        )


def band_fields(slots, lon_cells):
    rows = slots.shape[1] // 2
    marks = slots[:, rows, TLON - 1].astype(jnp.int32)
    vmem = pl.BlockSpec(memory_space=pltpu.VMEM)
    return pl.pallas_call(
        field_kernel,
        in_specs=[pl.BlockSpec(memory_space=pltpu.SMEM), vmem],
        out_specs=[vmem, vmem],
        out_shape=[
            jax.ShapeDtypeStruct((2, rows, lon_cells), jnp.float32),
            jax.ShapeDtypeStruct((rows, lon_cells), jnp.float32),
        ],
        scratch_shapes=[pltpu.SMEM((2 * lon_cells // TLON,), jnp.int32)],
        compiler_params=pltpu.CompilerParams(vmem_limit_bytes=16 * 2**20),
        cost_estimate=pl.CostEstimate(
            flops=rows * lon_cells * 8, bytes_accessed=rows * lon_cells * 24, transcendentals=0
        ),
    )(marks, slots)


def observation_slots(tiles, counts, index, value, weight, var_count, lev_count, row_count):
    slots = tile_sums(tiles, counts, index, value, weight, var_count, lev_count, row_count)
    mine, other = core_split(slots.transpose(1, 0, 2, 3))
    return jnp.concatenate([mine[0], core_swap(other)[0]], axis=0)


def pull_columns(weight, odd_weight, cells):
    lon = cells.shape[-1]
    odd = odd_weight * (0.5 * (cells + pltpu.roll(cells, lon - 1, cells.ndim - 1)))
    return weight * cells + 0.5 * (odd + pltpu.roll(odd, 1, cells.ndim - 1))


def observe_kernel(
    flag_ref, inc_ref, first_ref, second_ref, weight_ref, pull_ref, rim_first_ref, rim_second_ref, out_ref
):
    even = flag_ref[EVEN] == 1
    has_below, has_above = flag_ref[HAS_BELOW] == 1, flag_ref[HAS_ABOVE] == 1
    levels, rows, lon = inc_ref.shape
    first, second = first_ref[...], second_ref[...]
    lowest = jnp.concatenate([inc_ref[lev, 0:1] for lev in range(levels)], axis=0)
    highest = jnp.concatenate([inc_ref[lev, rows - 1 : rows] for lev in range(levels)], axis=0)
    below = jnp.where(has_below, jnp.where(even, second, first), lowest)
    above = jnp.where(has_above, jnp.where(even, first, second), highest)
    rim_below = [jnp.where(even, rim_second_ref[i], rim_first_ref[i]) for i in range(3)]
    rim_above = [jnp.where(even, rim_first_ref[i], rim_second_ref[i]) for i in range(3)]
    odd_below = pull_columns(rim_below[0], rim_below[1], 0.75 * below + 0.25 * lowest) - rim_below[2]
    even_above = pull_columns(rim_above[0], rim_above[1], 0.75 * above + 0.25 * highest) - rim_above[2]
    row = lax.broadcasted_iota(jnp.int32, (rows, lon), 0)
    for lev in range(levels):
        cells = inc_ref[lev]
        down = jnp.where(row == 0, below[lev : lev + 1], pltpu.roll(cells, 1, 0))
        up = jnp.where(row == rows - 1, above[lev : lev + 1], pltpu.roll(cells, rows - 1, 0))
        low = pull_columns(weight_ref[0, 0, lev], weight_ref[1, 0, lev], 0.75 * cells + 0.25 * down) - pull_ref[0, lev]
        high = pull_columns(weight_ref[0, 1, lev], weight_ref[1, 1, lev], 0.75 * cells + 0.25 * up) - pull_ref[1, lev]
        from_below = jnp.where(has_below, odd_below[lev : lev + 1], low[0:1])
        from_above = jnp.where(has_above, even_above[lev : lev + 1], high[rows - 1 : rows])
        high_down = jnp.where(row == 0, from_below, pltpu.roll(high, 1, 0))
        low_up = jnp.where(row == rows - 1, from_above, pltpu.roll(low, rows - 1, 0))
        out_ref[lev] = 0.75 * (low + high) + 0.25 * (high_down + low_up)


def row_groups(lines):
    starts = list(range(0, lines - 7, 8))
    return starts if starts[-1] + 8 == lines else starts + [lines - 8]


def strided(ref, chunk, start, rows):
    return ref[chunk, pl.ds(start, 8, stride=rows), :]


def to_chunks(ref, cells):
    for chunk in range(ref.shape[0]):
        ref[chunk] = cells[:, chunk * LANES : (chunk + 1) * LANES]


def spread_rows(cells, coef_ref, base, taps):
    out = []
    for row in range(len(cells) - taps + 1):
        total = coef_ref[base + row * taps] * cells[row]
        for tap in range(1, taps):
            total += coef_ref[base + row * taps + tap] * cells[row + tap]
        out.append(total)
    return out


def pull_rows(cells, coef_ref, base, taps):
    out = []
    for row in range(len(cells) - taps + 1):
        total = coef_ref[base + row * taps] * cells[row + taps - 1]
        for tap in range(1, taps):
            total += coef_ref[base + row * taps + tap] * cells[row + taps - 1 - tap]
        out.append(total)
    return out


def sum_members(spread_ref, zonal_ref, members_ref, inc_ref):
    size, variables, levels, rows, lon = members_ref.shape
    spread = jnp.concatenate(
        [spread_ref[chunk].astype(jnp.bfloat16) for chunk in range(spread_ref.shape[0])], axis=1
    )
    wide = LANES * 3 if lon % (LANES * 3) == 0 else LANES
    for start in range(0, lon, wide):
        lanes = slice(start, start + wide)
        localized = jnp.dot(spread, zonal_ref[:, lanes], preferred_element_type=jnp.float32)
        localized = localized.reshape(size, levels, rows, wide)
        for var in range(variables):
            total = members_ref[0, var, :, :, lanes].astype(jnp.float32) * localized[0]
            for k in range(1, size):
                total += members_ref[k, var, :, :, lanes].astype(jnp.float32) * localized[k]
            inc_ref[var, :, :, lanes] = total


def edge_kernel(alpha_ref, first_ref, second_ref):
    even = lax.rem(lax.axis_index("lat"), 2) == 0
    lines, rows = alpha_ref.shape[:2]
    half = first_ref.shape[0] // lines

    def step(pair, carry):
        one, two = alpha_ref[2 * pair], alpha_ref[2 * pair + 1]
        here = pl.ds(pl.multiple_of(pair * 2 * half, 8), 2 * half)
        head = jnp.concatenate([one[:half], two[:half]], axis=0)
        tail = jnp.concatenate([one[rows - half :], two[rows - half :]], axis=0)
        first_ref[here, :] = jnp.where(even, tail, head)
        second_ref[here, :] = jnp.where(even, head, tail)
        return carry

    lax.fori_loop(0, lines // 2, step, 0, unroll=2)


def forward_kernel(
    flag_ref,
    coef_ref,
    own_ref,
    first_ref,
    second_ref,
    zonal_ref,
    members_from,
    inc_ref,
    below_ref,
    above_ref,
    spread_ref,
    members_ref,
    arrived,
):
    copy = pltpu.make_async_copy(members_from, members_ref, arrived)
    copy.start()
    rows = members_ref.shape[3]
    half_band = first_ref.shape[0] * rows // own_ref.shape[1]
    taps = 2 * half_band + 1
    even = flag_ref[EVEN] == 1
    first = jnp.where(flag_ref[HAS_FIRST] == 1, first_ref[...], 0.0)
    second = jnp.where(flag_ref[HAS_SECOND] == 1, second_ref[...], 0.0)
    to_chunks(below_ref, jnp.where(even, second, first))
    to_chunks(above_ref, jnp.where(even, first, second))

    def step(chunk, carry):
        for start in row_groups(own_ref.shape[1] // rows):
            cells = wide_rows(own_ref, below_ref, above_ref, chunk, start, rows, half_band)
            for r, total in enumerate(spread_rows(cells, coef_ref, 0, taps)):
                spread_ref[chunk, pl.ds(start * rows + r, 8, stride=rows), :] = total
        return carry

    lax.fori_loop(0, own_ref.shape[0], step, 0)
    copy.wait()
    sum_members(spread_ref, zonal_ref, members_ref, inc_ref)


def wide_rows(own_ref, below_ref, above_ref, chunk, start, rows, half_band):
    below = [strided(below_ref, chunk, start * half_band + r, half_band) for r in range(half_band)]
    own = [strided(own_ref, chunk, start * rows + r, rows) for r in range(rows)]
    above = [strided(above_ref, chunk, start * half_band + r, half_band) for r in range(half_band)]
    return below + own + above


def weigh(part_ref, core, mine_ref, other_ref, weighted_ref, place, there):
    size, _, levels, rows, lon = part_ref.shape
    flat = levels * rows

    def step(k, carry):
        total = part_ref[k, core].astype(jnp.float32) * mine_ref[...]
        total += part_ref[k, 1 - core].astype(jnp.float32) * other_ref[...]
        if there is not None:
            total = jnp.where(there, total, 0.0)
        at = pl.multiple_of(place + k * flat, 16)
        weighted_ref[pl.ds(at, flat), :] = total.reshape(flat, lon).astype(jnp.bfloat16)
        return carry

    lax.fori_loop(0, size, step, 0)


def zonal_back(weighted_ref, zonal_ref, back_ref, lines):
    lon = zonal_ref.shape[0]
    wide = LANES * 3 if lon % (LANES * 3) == 0 else LANES
    for first in range(0, back_ref.shape[1], lines):
        here = slice(first, first + lines)
        weighted = weighted_ref[here, :]
        for start in range(0, lon, wide):
            back = lax.dot_general(
                weighted,
                zonal_ref[start : start + wide, :],
                (((1,), (1,)), ((), ())),
                preferred_element_type=jnp.float32,
            )
            for part in range(wide // LANES):
                back_ref[start // LANES + part, here, :] = back[:, part * LANES : (part + 1) * LANES]


def own_kernel(flag_ref, zonal_ref, mine_ref, other_ref, members_ref, back_ref, weighted_ref):
    weigh(members_ref, flag_ref[CORE], mine_ref, other_ref, weighted_ref, 0, None)
    zonal_back(weighted_ref, zonal_ref, back_ref, back_ref.shape[1])


def partner_back(flag_ref, zonal_ref, adjoints, partners, weighted_ref, back_ref):
    lines = back_ref.shape[1] // 2
    even, core = flag_ref[EVEN], flag_ref[CORE]
    half = len(partners) // 2
    for number, (place, flag) in enumerate((((even * lines), HAS_FIRST), ((1 - even) * lines, HAS_SECOND))):
        for part_ref in partners[number * half : (number + 1) * half]:
            mine_ref, other_ref = adjoints[2 * number : 2 * number + 2]
            weigh(part_ref, core, mine_ref, other_ref, weighted_ref, place, flag_ref[flag] == 1)
            place += part_ref.shape[0] * part_ref.shape[2] * part_ref.shape[3]
    zonal_back(weighted_ref, zonal_ref, back_ref, lines)


def back_rows(own_ref, partner_ref, chunk, start, rows, halo):
    lines = own_ref.shape[1]
    out = []
    for at in range(rows - halo, 2 * rows + halo):
        ref = own_ref if rows <= at < 2 * rows else partner_ref
        out.append(strided(ref, chunk, (lines if at >= 2 * rows else 0) + start * rows + at % rows, rows))
    return out


def between_kernel(rows, parts, *refs):
    flag_ref, coef_ref, own_ref, below_ref, above_ref, zonal_ref, own_back_ref = refs[:7]
    adjoints = refs[7:11]
    members_ref = refs[11]
    partners = refs[12 : 12 + 2 * parts]
    inc_ref, current_ref, weighted_ref, back_ref, spread_ref = refs[12 + 2 * parts :]
    lines = own_ref.shape[1]
    half_band = below_ref.shape[1] * rows // lines
    taps = 2 * half_band + 1
    partner_back(flag_ref, zonal_ref, adjoints, partners, weighted_ref, back_ref)

    def step(chunk, carry):
        for start in row_groups(lines // rows):
            back = back_rows(own_back_ref, back_ref, chunk, start, rows, 2 * half_band)
            pulled = pull_rows(back, coef_ref, rows * taps, taps)
            cells = wide_rows(own_ref, below_ref, above_ref, chunk, start, rows, half_band)
            cells = [c - step_size * (c + p) for c, p in zip(cells, pulled)]
            for r in range(rows):
                current_ref[chunk, pl.ds(start * rows + r, 8, stride=rows), :] = cells[half_band + r]
            for r, total in enumerate(spread_rows(cells, coef_ref, 0, taps)):
                spread_ref[chunk, pl.ds(start * rows + r, 8, stride=rows), :] = total
        return carry

    lax.fori_loop(0, own_ref.shape[0], step, 0)
    sum_members(spread_ref, zonal_ref, members_ref, inc_ref)


def last_kernel(rows, parts, taps, *refs):
    flag_ref, coef_ref, own_ref, zonal_ref, own_back_ref = refs[:5]
    adjoints = refs[5:9]
    partners = refs[9 : 9 + 2 * parts]
    out_ref, weighted_ref, back_ref, current_ref = refs[9 + 2 * parts :]
    half_band = taps // 2
    partner_back(flag_ref, zonal_ref, adjoints, partners, weighted_ref, back_ref)

    def step(chunk, carry):
        for start in row_groups(own_ref.shape[1] // rows):
            back = back_rows(own_back_ref, back_ref, chunk, start, rows, half_band)
            for r, pulled in enumerate(pull_rows(back, coef_ref, (rows + half_band) * taps, taps)):
                here = pl.ds(start * rows + r, 8, stride=rows)
                cell = own_ref[chunk, here, :]
                current_ref[chunk, here, :] = cell - step_size * (cell + pulled)
        return carry

    lax.fori_loop(0, own_ref.shape[0], step, 0)
    for chunk in range(own_ref.shape[0]):
        out_ref[:, chunk * LANES : (chunk + 1) * LANES] = current_ref[chunk]


def call(kernel, operands, outs, scratch, flops, anywhere=0, budget=20 * 2**20):
    vmem = pl.BlockSpec(memory_space=pltpu.VMEM)
    moved = sum(int(np.prod(x.shape)) * x.dtype.itemsize for x in list(operands) + list(outs))
    return pl.pallas_call(
        kernel,
        in_specs=[pl.BlockSpec(memory_space=pltpu.SMEM)] + [vmem] * (len(operands) - 1 - anywhere)
        + [pl.BlockSpec(memory_space=pl.ANY)] * anywhere,
        out_specs=[vmem] * len(outs),
        out_shape=list(outs),
        scratch_shapes=list(scratch),
        compiler_params=pltpu.CompilerParams(vmem_limit_bytes=budget),
        cost_estimate=pl.CostEstimate(flops=flops, bytes_accessed=moved, transcendentals=0),
    )(*operands)


def setup_kernel(rows, coef_ref, alpha_ref, out_ref, own_ref):
    to_chunks(own_ref, alpha_ref[...])
    count, taps = coef_ref.shape
    half_band = taps // 2
    first = lax.axis_index("lat") * rows

    def write(place, row, tap, on_grid):
        value = jnp.where(on_grid, coef_ref[jnp.clip(row, 0, count - 1), tap], 0.0)
        out_ref[place] = jnp.full(out_ref.shape[1:], value, jnp.float32)

    def forward(row, carry):
        for tap in range(taps):
            write(row * taps + tap, first + row, tap, True)
        return carry

    def backward(row, carry):
        target = first + row - half_band
        for tap in range(taps):
            source = target + half_band - tap
            on_grid = (target >= 0) & (target < count) & (source >= 0) & (source < count)
            write((rows + row) * taps + tap, source, tap, on_grid)
        return carry

    lax.fori_loop(0, rows, forward, 0)
    lax.fori_loop(0, rows + 2 * half_band, backward, 0)


def setup(merid_coef, own, rows):
    taps = merid_coef.shape[1]
    shape = ((2 * rows + taps - 1) * taps, 8, LANES)
    lines, lon = own.shape
    vmem = pl.BlockSpec(memory_space=pltpu.VMEM)
    return pl.pallas_call(
        functools.partial(setup_kernel, rows),
        in_specs=[pl.BlockSpec(memory_space=pltpu.SMEM), vmem],
        out_specs=[vmem, vmem],
        out_shape=[
            jax.ShapeDtypeStruct(shape, jnp.float32),
            jax.ShapeDtypeStruct((lon // LANES, lines, LANES), jnp.float32),
        ],
        compiler_params=pltpu.CompilerParams(vmem_limit_bytes=8 * 2**20),
        cost_estimate=pl.CostEstimate(flops=0, bytes_accessed=shape[0] * 4096 + 8 * own.size, transcendentals=0),
    )(merid_coef, own)


def band_setup(held, lev_count, rows, lon_cells):
    weights, pulls = band_fields(held, lon_cells)
    weights = weights.reshape(2, 2, lev_count, rows, lon_cells)
    pulls = pulls.reshape(2, lev_count, rows, lon_cells)
    rims = band_swap(
        *by_partner(
            jnp.concatenate([weights[:, 0, :, 0], pulls[None, 0, :, 0]]),
            jnp.concatenate([weights[:, 1, :, -1], pulls[None, 1, :, -1]]),
        )
    )
    return weights, pulls, rims


def body(
    members, alpha, zonal_loc, merid_coef, slot_tile, obs_count, obs_index, obs_value, obs_weight
):
    half_band = merid_coef.shape[1] // 2
    _, var_count, lev_count, rows, lon_cells = members.shape
    slot_count = slot_tile.shape[-1]

    members_per = members.shape[0]
    lines = members_per * lev_count * rows
    even, has_below, has_above = band_sides()
    first_there = jnp.where(even, has_above, has_below)
    second_there = jnp.where(even, has_below, has_above)
    core = lax.axis_index("mem") % 2
    flags = jnp.stack(
        [x.astype(jnp.int32) for x in (even, core, first_there, second_there, has_below, has_above)]
    )

    edge_lines = members_per * lev_count * half_band
    edge_shape = jax.ShapeDtypeStruct((edge_lines, lon_cells), jnp.float32)
    vmem = pl.BlockSpec(memory_space=pltpu.VMEM)
    sends = pl.pallas_call(
        edge_kernel,
        in_specs=[vmem],
        out_specs=[vmem, vmem],
        out_shape=[edge_shape, edge_shape],
        compiler_params=pltpu.CompilerParams(vmem_limit_bytes=8 * 2**20),
        cost_estimate=pl.CostEstimate(flops=0, bytes_accessed=16 * edge_lines * lon_cells, transcendentals=0),
    )(alpha.reshape(-1, rows, lon_cells))
    obs_index, obs_value, obs_weight, sends = lax.optimization_barrier((obs_index, obs_value, obs_weight, sends))
    halo_first, halo_second = band_swap(*sends)
    coeffs, own = setup(merid_coef, alpha.reshape(lines, lon_cells), rows)

    total_share = sum(share for share, _ in PARTS)
    cuts = [sum(share for share, _ in PARTS[:i]) * members_per // total_share for i in range(len(PARTS) + 1)]
    pieces = [(x, y, event) for x, y, (_, event) in zip(cuts[:-1], cuts[1:], PARTS) if x < y]
    parts = [members[x:y] for x, y, _ in pieces]

    held = observation_slots(
        slot_tile.reshape(-1),
        obs_count.reshape(-1),
        obs_index.reshape(slot_count, -1),
        obs_value.reshape(slot_count, -1),
        obs_weight.reshape(slot_count, -1),
        var_count,
        lev_count,
        rows,
    )
    steps = chip_steps()
    for number, perm in enumerate(steps):
        if number == len(steps) - 1:
            halo_first, halo_second, held, coeffs, own, parts = lax.optimization_barrier(
                (halo_first, halo_second, held, coeffs, own, parts)
            )
        held = jnp.concatenate([held, lax.ppermute(held, "mem", perm)], axis=0)
    fetched = [band_swap(part, part) for part in parts]

    def pin(value, event):
        for number, (_, _, name) in enumerate(pieces):
            if name == event:
                value, fetched[number] = lax.optimization_barrier((value, fetched[number]))
        return value

    inc_shape = jax.ShapeDtypeStruct((var_count, lev_count, rows, lon_cells), jnp.float32)
    line_shape = jax.ShapeDtypeStruct((lines, lon_cells), jnp.float32)
    chunks = lon_cells // LANES
    chunk_shape = jax.ShapeDtypeStruct((chunks, lines, LANES), jnp.float32)
    halo_shape = jax.ShapeDtypeStruct((chunks, halo_first.shape[0], LANES), jnp.float32)
    zonal_flops = 2 * lines * lon_cells * lon_cells
    chunk_scratch = pltpu.VMEM((chunks, lines, LANES), jnp.float32)
    weighted_scratch = pltpu.VMEM((2 * lines, lon_cells), jnp.bfloat16)
    back_scratch = pltpu.VMEM((chunks, 2 * lines, LANES), jnp.float32)
    partial_value, below, above = call(
        forward_kernel,
        (flags, coeffs, own, halo_first, halo_second, zonal_loc, members),
        [inc_shape, halo_shape, halo_shape],
        [chunk_scratch, pltpu.VMEM(members.shape, members.dtype), pltpu.SemaphoreType.DMA],
        zonal_flops,
        anywhere=1,
    )
    partial_value = pin(partial_value, "forward")
    for iteration in range(ITERS):
        mine, other = core_split(partial_value)
        inc = mine + core_swap(other)
        for number, perm in enumerate(steps):
            inc = inc + lax.ppermute(inc, "mem", perm)
            if iteration == 0 and number == 0:
                inc, held = lax.optimization_barrier((inc, held))
                weights, pulls, rims = band_setup(held, lev_count, rows, lon_cells)
            if iteration == 0 and number == len(steps) - 1:
                inc, rims = lax.optimization_barrier((inc, rims))
            if iteration == 0:
                inc = pin(inc, f"chip{number}")
        inc = inc[0]
        edges = band_swap(*by_partner(inc[:, 0], inc[:, -1]))
        (adjoint,) = call(
            observe_kernel,
            (flags, inc, *edges, weights, pulls, *rims),
            [jax.ShapeDtypeStruct(inc.shape, jnp.float32)],
            [],
            40 * 2 * inc.size,
        )
        if iteration == 0:
            adjoint = pin(adjoint, "adjoint")
        first, second = band_swap(adjoint, adjoint)
        other = core_swap(adjoint)
        (own_back,) = call(
            own_kernel,
            (flags, zonal_loc, adjoint, other, members),
            [chunk_shape],
            [pltpu.VMEM((lines, lon_cells), jnp.bfloat16)],
            zonal_flops,
        )
        first, second, own_back = lax.optimization_barrier((first, second, own_back))
        halves = (first, core_swap(first), second, core_swap(second))
        partners = [x[0] for x in fetched] + [x[1] for x in fetched]
        if iteration + 1 < ITERS:
            partial_value, own = call(
                functools.partial(between_kernel, rows, len(pieces)),
                (flags, coeffs, own, below, above, zonal_loc, own_back, *halves, members, *partners),
                [inc_shape, chunk_shape],
                [weighted_scratch, back_scratch, chunk_scratch],
                3 * zonal_flops,
            )
        else:
            (own,) = call(
                functools.partial(last_kernel, rows, len(pieces), 2 * half_band + 1),
                (flags, coeffs, own, zonal_loc, own_back, *halves, *partners),
                [line_shape],
                [weighted_scratch, back_scratch, chunk_scratch],
                2 * zonal_flops,
            )
    return own.reshape(alpha.shape)


def solution(mesh):
    in_specs = (
        P("mem", None, None, "lat", None),
        P("mem", None, "lat", None),
        P(),
        P(),
        P("lat", "mem", None),
        P("lat", "mem", None),
        P("lat", "mem", None, None),
        P("lat", "mem", None, None),
        P("lat", "mem", None, None),
    )
    out_specs = P("mem", None, "lat", None)
    return jax.shard_map(body, mesh=mesh, in_specs=in_specs, out_specs=out_specs, check_vma=False)
```

```python
import functools

import jax
import jax.numpy as jnp
import numpy as np
from jax import lax
from jax.experimental import pallas as pl
from jax.experimental.pallas import tpu as pltpu
from jax.sharding import PartitionSpec as P

TLON = 128
ITERS = 2
LANES = 128
OBS_CHUNK = 1024
EVEN, CORE, HAS_FIRST, HAS_SECOND, HAS_BELOW, HAS_ABOVE = range(6)


step_size = 0.3


def band_pairs(second):
    bands, groups = lax.axis_size("lat"), lax.axis_size("mem")
    perm = []
    for group in range(groups):
        for band in range(bands):
            other = ((band + second) ^ 1) - second
            if 0 <= other < bands:
                target = group * bands + other
            else:
                target = (group ^ 1) * bands + band
            perm.append((group * bands + band, target))
    return perm


def band_swap(send_first, send_second):
    axes = ("mem", "lat")
    return (
        lax.ppermute(send_first, axes, band_pairs(0)),
        lax.ppermute(send_second, axes, band_pairs(1)),
    )


def band_sides():
    band = lax.axis_index("lat")
    return band % 2 == 0, band > 0, band < lax.axis_size("lat") - 1


def by_partner(to_prev, to_next):
    even, _, _ = band_sides()
    return jnp.where(even, to_next, to_prev), jnp.where(even, to_prev, to_next)


def core_swap(cells):
    count = lax.axis_size("mem")
    return lax.ppermute(cells, "mem", [(i, i ^ 1) for i in range(count)])


def chip_steps():
    count = lax.axis_size("mem")
    bits = [1 << b for b in range(1, count.bit_length() - 1)]
    return [
        [(i, i ^ bits[(step + i % 2) % len(bits)]) for i in range(count)]
        for step in range(len(bits))
    ]


def core_split(cells):
    core = lax.axis_index("mem") % 2
    half = cells.shape[0] // 2
    mine = lax.dynamic_slice_in_dim(cells, core * half, half, 0)
    other = lax.dynamic_slice_in_dim(cells, (1 - core) * half, half, 0)
    return mine, other


def split_two(x):
    top = x.astype(jnp.bfloat16)
    return top, (x - top.astype(jnp.float32)).astype(jnp.bfloat16)


def tile_kernel(tile_ref, count_ref, row_ref, lane_ref, index_ref, value_ref, weight_ref, out_ref):
    slot = pl.program_id(0)
    count = count_ref[slot]
    half = TLON // 2
    wide = half + 8
    rows = row_ref.shape[0]
    out_ref[...] = jnp.zeros_like(out_ref)
    spots = row_ref[...]
    lanes = lane_ref[...]
    coarse = 2 * lax.broadcasted_iota(jnp.int32, (wide, 1), 0)
    chunk = min(OBS_CHUNK, index_ref.shape[-1])

    def step(part, carry):
        @pl.when(part * chunk < count)
        def _():
            here = pl.ds(pl.multiple_of(part * chunk, chunk), chunk)
            index = index_ref[0, :, here]
            weight = weight_ref[0, :, here]
            place = lax.broadcasted_iota(jnp.int32, (1, chunk), 1) + part * chunk
            weight = jnp.where(place < count, weight, 0.0)
            pull = weight * value_ref[0, :, here]
            high = lax.shift_right_logical(index, TLON.bit_length() - 1)
            low = lax.bitwise_and(index, TLON - 1)
            at_row = jnp.where(spots == high, 1.0, 0.0).astype(jnp.bfloat16)
            contract = (((1,), (1,)), ((), ()))
            total = jnp.zeros((rows, TLON), jnp.float32)
            for piece in split_two(weight):
                at_lane = jnp.where(lanes == low, piece.astype(jnp.float32), 0.0)
                total += lax.dot_general(
                    at_row, at_lane.astype(jnp.bfloat16), contract, preferred_element_type=jnp.float32
                )
            apart = jnp.abs(low - coarse)
            share = jnp.where(apart == 0, 1.0, jnp.where(apart == 1, 0.5, 0.0))
            pulled = jnp.zeros((rows, wide), jnp.float32)
            for piece in split_two(pull):
                at_coarse = share * piece.astype(jnp.float32)
                pulled += lax.dot_general(
                    at_row, at_coarse.astype(jnp.bfloat16), contract, preferred_element_type=jnp.float32
                )
            pulled = jnp.concatenate(
                [pulled, jnp.zeros((rows, TLON - wide), jnp.float32)], axis=1
            )
            groups = out_ref.shape[1]
            step_rows = rows // groups
            for group in range(groups):
                mine = slice(group * step_rows, (group + 1) * step_rows)
                out_ref[0, group, :step_rows] += total[mine]
                out_ref[0, group, step_rows:] += pulled[mine]

        return carry

    lax.fori_loop(0, index_ref.shape[-1] // chunk, step, 0)
    step_rows = rows // out_ref.shape[1]
    marker = jnp.where(count > 0, tile_ref[slot] + 1, 0).astype(jnp.float32)
    lane = lax.broadcasted_iota(jnp.int32, (8, TLON), 1)
    for group in range(out_ref.shape[1]):
        block = out_ref[0, group, step_rows : step_rows + 8]
        out_ref[0, group, step_rows : step_rows + 8] = jnp.where(lane == TLON - 1, marker, block)


def tile_sums(tiles, counts, index, value, weight, var_count, lev_count, row_count):
    slots, length = index.shape
    var, par, lev, row = np.meshgrid(
        np.arange(var_count), np.arange(2), np.arange(lev_count), np.arange(row_count), indexing="ij"
    )
    spot = ((var * lev_count + lev) * row_count + row) * 2 + par
    spot = spot.reshape(-1, 1).astype(np.int32)
    lanes = np.arange(TLON).reshape(2, TLON // 2)
    lanes = (2 * (lanes % (TLON // 2)) + lanes // (TLON // 2)).reshape(-1, 1).astype(np.int32)
    rows = spot.shape[0]
    whole = lambda shape: pl.BlockSpec(shape, lambda s, *_: (0,) * len(shape))
    line = pl.BlockSpec((1, 1, length), lambda s, *_: (s, 0, 0))
    out = (slots, var_count, 2 * rows // var_count, TLON)
    return pl.pallas_call(
        tile_kernel,
        grid_spec=pltpu.PrefetchScalarGridSpec(
            num_scalar_prefetch=2,
            grid=(slots,),
            in_specs=[whole(spot.shape), whole(lanes.shape), line, line, line],
            out_specs=pl.BlockSpec((1,) + out[1:], lambda s, *_: (s, 0, 0, 0)),
        ),
        out_shape=jax.ShapeDtypeStruct(out, jnp.float32),
        compiler_params=pltpu.CompilerParams(vmem_limit_bytes=16 * 2**20),
        cost_estimate=pl.CostEstimate(
            flops=2 * slots * length * rows * 400, bytes_accessed=slots * rows * 1024, transcendentals=0
        ),
    )(
        tiles,
        counts,
        jnp.asarray(spot),
        jnp.asarray(lanes),
        index[:, None],
        value[:, None],
        weight[:, None],
    )


def field_kernel(mark_ref, *refs):
    groups = refs[:-3]
    weight_ref, pull_ref, where_ref = refs[-3:]
    tile_count = where_ref.shape[0]
    half = TLON // 2
    size, rows = groups[0].shape[0], weight_ref.shape[1]

    def note(slot, carry):
        mark = mark_ref[slot]

        @pl.when(mark > 0)
        def _():
            where_ref[mark - 1] = slot

        return carry

    def tile_rows(slot, here):
        at = lax.rem(slot, size)
        out = groups[0][at, here]
        for number in range(1, len(groups)):
            out = jnp.where(slot >= number * size, groups[number][at, here], out)
        return out

    for tile in range(tile_count):
        where_ref[tile] = 0
    lax.fori_loop(0, mark_ref.shape[0], note, 0)
    lane = lax.broadcasted_iota(jnp.int32, (rows, TLON), 1)
    upper, lower = slice(0, rows), slice(rows, 2 * rows)
    for pair in range(tile_count // 2):
        left = where_ref[2 * pair]
        right = where_ref[2 * pair + 1]
        before = where_ref[(2 * pair - 1) % tile_count]
        here = slice(pair * TLON, (pair + 1) * TLON)
        first, second = tile_rows(left, upper), tile_rows(right, upper)
        weight_ref[0, :, here] = jnp.where(lane < half, first, pltpu.roll(second, half, 1))
        weight_ref[1, :, here] = jnp.where(lane < half, pltpu.roll(first, half, 1), second)
        first, second, third = tile_rows(left, lower), tile_rows(right, lower), tile_rows(before, lower)
        pull_ref[:, here] = (
            jnp.where(lane <= half, first, 0.0)
            + jnp.where(lane >= half, pltpu.roll(second, half, 1), 0.0)
            + jnp.where(lane == 0, pltpu.roll(third, half, 1), 0.0)
        )


def band_fields(held, lon_cells):
    rows = held[0].shape[1] // 2
    marks = jnp.concatenate([slots[:, rows, TLON - 1] for slots in held]).astype(jnp.int32)
    vmem = pl.BlockSpec(memory_space=pltpu.VMEM)
    return pl.pallas_call(
        field_kernel,
        in_specs=[pl.BlockSpec(memory_space=pltpu.SMEM)] + [vmem] * len(held),
        out_specs=[vmem, vmem],
        out_shape=[
            jax.ShapeDtypeStruct((2, rows, lon_cells), jnp.float32),
            jax.ShapeDtypeStruct((rows, lon_cells), jnp.float32),
        ],
        scratch_shapes=[pltpu.SMEM((2 * lon_cells // TLON,), jnp.int32)],
        compiler_params=pltpu.CompilerParams(vmem_limit_bytes=16 * 2**20),
        cost_estimate=pl.CostEstimate(
            flops=rows * lon_cells * 8, bytes_accessed=rows * lon_cells * 24, transcendentals=0
        ),
    )(marks, *held)


def observation_slots(tiles, counts, index, value, weight, var_count, lev_count, row_count):
    slots = tile_sums(tiles, counts, index, value, weight, var_count, lev_count, row_count)
    mine, other = core_split(slots.transpose(1, 0, 2, 3))
    return jnp.concatenate([mine[0], core_swap(other)[0]], axis=0)


def pull_columns(weight, odd_weight, cells):
    lon = cells.shape[-1]
    odd = odd_weight * (0.5 * (cells + pltpu.roll(cells, lon - 1, cells.ndim - 1)))
    return weight * cells + 0.5 * (odd + pltpu.roll(odd, 1, cells.ndim - 1))


def observe_kernel(
    flag_ref, inc_ref, first_ref, second_ref, weight_ref, pull_ref, rim_first_ref, rim_second_ref, out_ref
):
    even = flag_ref[EVEN] == 1
    has_below, has_above = flag_ref[HAS_BELOW] == 1, flag_ref[HAS_ABOVE] == 1
    levels, rows, lon = inc_ref.shape
    first, second = first_ref[first_ref.shape[0] - 1], second_ref[second_ref.shape[0] - 1]
    lowest = jnp.concatenate([inc_ref[lev, 0:1] for lev in range(levels)], axis=0)
    highest = jnp.concatenate([inc_ref[lev, rows - 1 : rows] for lev in range(levels)], axis=0)
    below = jnp.where(has_below, jnp.where(even, second, first), lowest)
    above = jnp.where(has_above, jnp.where(even, first, second), highest)
    rim_below = [jnp.where(even, rim_second_ref[i], rim_first_ref[i]) for i in range(3)]
    rim_above = [jnp.where(even, rim_first_ref[i], rim_second_ref[i]) for i in range(3)]
    odd_below = pull_columns(rim_below[0], rim_below[1], 0.75 * below + 0.25 * lowest) - rim_below[2]
    even_above = pull_columns(rim_above[0], rim_above[1], 0.75 * above + 0.25 * highest) - rim_above[2]
    row = lax.broadcasted_iota(jnp.int32, (rows, lon), 0)
    for lev in range(levels):
        cells = inc_ref[lev]
        down = jnp.where(row == 0, below[lev : lev + 1], pltpu.roll(cells, 1, 0))
        up = jnp.where(row == rows - 1, above[lev : lev + 1], pltpu.roll(cells, rows - 1, 0))
        low = pull_columns(weight_ref[0, 0, lev], weight_ref[1, 0, lev], 0.75 * cells + 0.25 * down) - pull_ref[0, lev]
        high = pull_columns(weight_ref[0, 1, lev], weight_ref[1, 1, lev], 0.75 * cells + 0.25 * up) - pull_ref[1, lev]
        from_below = jnp.where(has_below, odd_below[lev : lev + 1], low[0:1])
        from_above = jnp.where(has_above, even_above[lev : lev + 1], high[rows - 1 : rows])
        high_down = jnp.where(row == 0, from_below, pltpu.roll(high, 1, 0))
        low_up = jnp.where(row == rows - 1, from_above, pltpu.roll(low, rows - 1, 0))
        out_ref[lev] = 0.75 * (low + high) + 0.25 * (high_down + low_up)


def row_groups(lines):
    starts = list(range(0, lines - 7, 8))
    return starts if starts[-1] + 8 == lines else starts + [lines - 8]


def strided(ref, chunk, start, rows):
    return ref[chunk, pl.ds(start, 8, stride=rows), :]


def to_chunks(ref, cells):
    for chunk in range(ref.shape[0]):
        ref[chunk] = cells[:, chunk * LANES : (chunk + 1) * LANES]


def spread_rows(cells, coef_ref, base, taps):
    out = []
    for row in range(len(cells) - taps + 1):
        total = coef_ref[base + row * taps] * cells[row]
        for tap in range(1, taps):
            total += coef_ref[base + row * taps + tap] * cells[row + tap]
        out.append(total)
    return out


def pull_rows(cells, coef_ref, base, taps):
    out = []
    for row in range(len(cells) - taps + 1):
        total = coef_ref[base + row * taps] * cells[row + taps - 1]
        for tap in range(1, taps):
            total += coef_ref[base + row * taps + tap] * cells[row + taps - 1 - tap]
        out.append(total)
    return out


def sum_members(core, spread_ref, zonal_ref, members_ref, mine_ref, other_ref):
    size, _, levels, rows, lon = members_ref.shape
    spread = jnp.concatenate(
        [spread_ref[chunk].astype(jnp.bfloat16) for chunk in range(spread_ref.shape[0])], axis=1
    )
    wide = LANES * 3 if lon % (LANES * 3) == 0 else LANES
    for start in range(0, lon, wide):
        lanes = slice(start, start + wide)
        localized = jnp.dot(spread, zonal_ref[:, lanes], preferred_element_type=jnp.float32)
        localized = localized.reshape(size, levels, rows, wide)
        for var, inc_ref in ((core, mine_ref), (1 - core, other_ref)):
            total = members_ref[0, var, :, :, lanes].astype(jnp.float32) * localized[0]
            for k in range(1, size):
                total += members_ref[k, var, :, :, lanes].astype(jnp.float32) * localized[k]
            inc_ref[:, :, lanes] = total


def edge_kernel(alpha_ref, first_ref, second_ref):
    even = lax.rem(lax.axis_index("lat"), 2) == 0
    lines, rows = alpha_ref.shape[:2]
    half = first_ref.shape[0] // lines

    def step(pair, carry):
        one, two = alpha_ref[2 * pair], alpha_ref[2 * pair + 1]
        here = pl.ds(pl.multiple_of(pair * 2 * half, 8), 2 * half)
        head = jnp.concatenate([one[:half], two[:half]], axis=0)
        tail = jnp.concatenate([one[rows - half :], two[rows - half :]], axis=0)
        first_ref[here, :] = jnp.where(even, tail, head)
        second_ref[here, :] = jnp.where(even, head, tail)
        return carry

    lax.fori_loop(0, lines // 2, step, 0, unroll=2)


def forward_kernel(
    flag_ref,
    coef_ref,
    own_ref,
    first_ref,
    second_ref,
    zonal_ref,
    members_from,
    mine_ref,
    other_ref,
    below_ref,
    above_ref,
    spread_ref,
    members_ref,
    arrived,
):
    copy = pltpu.make_async_copy(members_from, members_ref, arrived)
    copy.start()
    rows = members_ref.shape[3]
    half_band = first_ref.shape[0] * rows // own_ref.shape[1]
    taps = 2 * half_band + 1
    even = flag_ref[EVEN] == 1
    first = jnp.where(flag_ref[HAS_FIRST] == 1, first_ref[...], 0.0)
    second = jnp.where(flag_ref[HAS_SECOND] == 1, second_ref[...], 0.0)
    to_chunks(below_ref, jnp.where(even, second, first))
    to_chunks(above_ref, jnp.where(even, first, second))

    def step(chunk, carry):
        for start in row_groups(own_ref.shape[1] // rows):
            cells = wide_rows(own_ref, below_ref, above_ref, chunk, start, rows, half_band)
            for r, total in enumerate(spread_rows(cells, coef_ref, 0, taps)):
                spread_ref[chunk, pl.ds(start * rows + r, 8, stride=rows), :] = total
        return carry

    lax.fori_loop(0, own_ref.shape[0], step, 0)
    copy.wait()
    sum_members(flag_ref[CORE], spread_ref, zonal_ref, members_ref, mine_ref, other_ref)


def wide_rows(own_ref, below_ref, above_ref, chunk, start, rows, half_band):
    below = [strided(below_ref, chunk, start * half_band + r, half_band) for r in range(half_band)]
    own = [strided(own_ref, chunk, start * rows + r, rows) for r in range(rows)]
    above = [strided(above_ref, chunk, start * half_band + r, half_band) for r in range(half_band)]
    return below + own + above


def weigh(part_ref, core, mine_ref, other_ref, weighted_ref, place, there):
    size, _, levels, rows, lon = part_ref.shape
    flat = levels * rows

    def step(k, carry):
        total = part_ref[k, core].astype(jnp.float32) * mine_ref[...]
        total += part_ref[k, 1 - core].astype(jnp.float32) * other_ref[...]
        if there is not None:
            total = jnp.where(there, total, 0.0)
        at = pl.multiple_of(place + k * flat, 16)
        weighted_ref[pl.ds(at, flat), :] = total.reshape(flat, lon).astype(jnp.bfloat16)
        return carry

    lax.fori_loop(0, size, step, 0)


def zonal_back(weighted_ref, zonal_ref, back_ref, lines):
    lon = zonal_ref.shape[0]
    wide = LANES * 3 if lon % (LANES * 3) == 0 else LANES
    for first in range(0, back_ref.shape[1], lines):
        here = slice(first, first + lines)
        weighted = weighted_ref[here, :]
        for start in range(0, lon, wide):
            back = lax.dot_general(
                weighted,
                zonal_ref[start : start + wide, :],
                (((1,), (1,)), ((), ())),
                preferred_element_type=jnp.float32,
            )
            for part in range(wide // LANES):
                back_ref[start // LANES + part, here, :] = back[:, part * LANES : (part + 1) * LANES]


def own_kernel(flag_ref, zonal_ref, mine_ref, other_ref, members_ref, back_ref, weighted_ref):
    weigh(members_ref, flag_ref[CORE], mine_ref, other_ref, weighted_ref, 0, None)
    zonal_back(weighted_ref, zonal_ref, back_ref, back_ref.shape[1])


def partner_back(flag_ref, zonal_ref, adjoints, partners, weighted_ref, back_ref):
    lines = back_ref.shape[1] // 2
    even, core = flag_ref[EVEN], flag_ref[CORE]
    half = len(partners) // 2
    for number, (place, flag) in enumerate((((even * lines), HAS_FIRST), ((1 - even) * lines, HAS_SECOND))):
        for part_ref in partners[number * half : (number + 1) * half]:
            mine_ref, other_ref = adjoints[2 * number : 2 * number + 2]
            weigh(part_ref, core, mine_ref, other_ref, weighted_ref, place, flag_ref[flag] == 1)
            place += part_ref.shape[0] * part_ref.shape[2] * part_ref.shape[3]
    zonal_back(weighted_ref, zonal_ref, back_ref, lines)


def back_rows(own_ref, partner_ref, chunk, start, rows, halo):
    lines = own_ref.shape[1]
    out = []
    for at in range(rows - halo, 2 * rows + halo):
        ref = own_ref if rows <= at < 2 * rows else partner_ref
        out.append(strided(ref, chunk, (lines if at >= 2 * rows else 0) + start * rows + at % rows, rows))
    return out


def between_kernel(rows, parts, *refs):
    flag_ref, coef_ref, own_ref, below_ref, above_ref, zonal_ref, own_back_ref = refs[:7]
    adjoints = refs[7:11]
    members_ref = refs[11]
    partners = refs[12 : 12 + 2 * parts]
    mine_ref, other_ref, current_ref, weighted_ref, back_ref, spread_ref = refs[12 + 2 * parts :]
    lines = own_ref.shape[1]
    half_band = below_ref.shape[1] * rows // lines
    taps = 2 * half_band + 1
    partner_back(flag_ref, zonal_ref, adjoints, partners, weighted_ref, back_ref)

    def step(chunk, carry):
        for start in row_groups(lines // rows):
            back = back_rows(own_back_ref, back_ref, chunk, start, rows, 2 * half_band)
            pulled = pull_rows(back, coef_ref, rows * taps, taps)
            cells = wide_rows(own_ref, below_ref, above_ref, chunk, start, rows, half_band)
            cells = [c - step_size * (c + p) for c, p in zip(cells, pulled)]
            for r in range(rows):
                current_ref[chunk, pl.ds(start * rows + r, 8, stride=rows), :] = cells[half_band + r]
            for r, total in enumerate(spread_rows(cells, coef_ref, 0, taps)):
                spread_ref[chunk, pl.ds(start * rows + r, 8, stride=rows), :] = total
        return carry

    lax.fori_loop(0, own_ref.shape[0], step, 0)
    sum_members(flag_ref[CORE], spread_ref, zonal_ref, members_ref, mine_ref, other_ref)


def last_kernel(rows, parts, taps, *refs):
    flag_ref, coef_ref, own_ref, zonal_ref, own_back_ref = refs[:5]
    adjoints = refs[5:9]
    partners = refs[9 : 9 + 2 * parts]
    out_ref, weighted_ref, back_ref, current_ref = refs[9 + 2 * parts :]
    half_band = taps // 2
    partner_back(flag_ref, zonal_ref, adjoints, partners, weighted_ref, back_ref)

    def step(chunk, carry):
        for start in row_groups(own_ref.shape[1] // rows):
            back = back_rows(own_back_ref, back_ref, chunk, start, rows, half_band)
            for r, pulled in enumerate(pull_rows(back, coef_ref, (rows + half_band) * taps, taps)):
                here = pl.ds(start * rows + r, 8, stride=rows)
                cell = own_ref[chunk, here, :]
                current_ref[chunk, here, :] = cell - step_size * (cell + pulled)
        return carry

    lax.fori_loop(0, own_ref.shape[0], step, 0)
    for chunk in range(own_ref.shape[0]):
        out_ref[:, chunk * LANES : (chunk + 1) * LANES] = current_ref[chunk]


def call(kernel, operands, outs, scratch, flops, anywhere=0, budget=20 * 2**20):
    vmem = pl.BlockSpec(memory_space=pltpu.VMEM)
    moved = sum(int(np.prod(x.shape)) * x.dtype.itemsize for x in list(operands) + list(outs))
    return pl.pallas_call(
        kernel,
        in_specs=[pl.BlockSpec(memory_space=pltpu.SMEM)] + [vmem] * (len(operands) - 1 - anywhere)
        + [pl.BlockSpec(memory_space=pl.ANY)] * anywhere,
        out_specs=[vmem] * len(outs),
        out_shape=list(outs),
        scratch_shapes=list(scratch),
        compiler_params=pltpu.CompilerParams(vmem_limit_bytes=budget),
        cost_estimate=pl.CostEstimate(flops=flops, bytes_accessed=moved, transcendentals=0),
    )(*operands)


def setup_kernel(rows, coef_ref, alpha_ref, out_ref, own_ref):
    to_chunks(own_ref, alpha_ref[...])
    count, taps = coef_ref.shape
    half_band = taps // 2
    first = lax.axis_index("lat") * rows

    def write(place, row, tap, on_grid):
        value = jnp.where(on_grid, coef_ref[jnp.clip(row, 0, count - 1), tap], 0.0)
        out_ref[place] = jnp.full(out_ref.shape[1:], value, jnp.float32)

    def forward(row, carry):
        for tap in range(taps):
            write(row * taps + tap, first + row, tap, True)
        return carry

    def backward(row, carry):
        target = first + row - half_band
        for tap in range(taps):
            source = target + half_band - tap
            on_grid = (target >= 0) & (target < count) & (source >= 0) & (source < count)
            write((rows + row) * taps + tap, source, tap, on_grid)
        return carry

    lax.fori_loop(0, rows, forward, 0)
    lax.fori_loop(0, rows + 2 * half_band, backward, 0)


def setup(merid_coef, own, rows):
    taps = merid_coef.shape[1]
    shape = ((2 * rows + taps - 1) * taps, 8, LANES)
    lines, lon = own.shape
    vmem = pl.BlockSpec(memory_space=pltpu.VMEM)
    return pl.pallas_call(
        functools.partial(setup_kernel, rows),
        in_specs=[pl.BlockSpec(memory_space=pltpu.SMEM), vmem],
        out_specs=[vmem, vmem],
        out_shape=[
            jax.ShapeDtypeStruct(shape, jnp.float32),
            jax.ShapeDtypeStruct((lon // LANES, lines, LANES), jnp.float32),
        ],
        compiler_params=pltpu.CompilerParams(vmem_limit_bytes=8 * 2**20),
        cost_estimate=pl.CostEstimate(flops=0, bytes_accessed=shape[0] * 4096 + 8 * own.size, transcendentals=0),
    )(merid_coef, own)


def pack_kernel(flag_ref, inc_ref, weight_ref, pull_ref, first_ref, second_ref):
    even = flag_ref[EVEN] == 1
    levels, rows, _ = inc_ref.shape

    def line(ref, *place):
        return jnp.concatenate([ref[(*place[:-1], lev, slice(place[-1], place[-1] + 1))] for lev in range(levels)], axis=0)

    for number in range(4):
        if number < 2:
            low, high = line(weight_ref, number, 0, 0), line(weight_ref, number, 1, rows - 1)
        elif number == 2:
            low, high = line(pull_ref, 0, 0), line(pull_ref, 1, rows - 1)
        else:
            low, high = line(inc_ref, 0), line(inc_ref, rows - 1)
        first_ref[number] = jnp.where(even, high, low)
        second_ref[number] = jnp.where(even, low, high)


def body(
    members, alpha, zonal_loc, merid_coef, slot_tile, obs_count, obs_index, obs_value, obs_weight
):
    half_band = merid_coef.shape[1] // 2
    _, var_count, lev_count, rows, lon_cells = members.shape
    slot_count = slot_tile.shape[-1]

    members_per = members.shape[0]
    lines = members_per * lev_count * rows
    even, has_below, has_above = band_sides()
    first_there = jnp.where(even, has_above, has_below)
    second_there = jnp.where(even, has_below, has_above)
    core = lax.axis_index("mem") % 2
    flags = jnp.stack(
        [x.astype(jnp.int32) for x in (even, core, first_there, second_there, has_below, has_above)]
    )

    edge_lines = members_per * lev_count * half_band
    edge_shape = jax.ShapeDtypeStruct((edge_lines, lon_cells), jnp.float32)
    vmem = pl.BlockSpec(memory_space=pltpu.VMEM)
    sends = pl.pallas_call(
        edge_kernel,
        in_specs=[vmem],
        out_specs=[vmem, vmem],
        out_shape=[edge_shape, edge_shape],
        compiler_params=pltpu.CompilerParams(vmem_limit_bytes=8 * 2**20),
        cost_estimate=pl.CostEstimate(flops=0, bytes_accessed=16 * edge_lines * lon_cells, transcendentals=0),
    )(alpha.reshape(-1, rows, lon_cells))
    obs_index, obs_value, obs_weight, sends = lax.optimization_barrier((obs_index, obs_value, obs_weight, sends))
    halo_first, halo_second = band_swap(*sends)
    coeffs, own = setup(merid_coef, alpha.reshape(lines, lon_cells), rows)

    held = observation_slots(
        slot_tile.reshape(-1),
        obs_count.reshape(-1),
        obs_index.reshape(slot_count, -1),
        obs_value.reshape(slot_count, -1),
        obs_weight.reshape(slot_count, -1),
        var_count,
        lev_count,
        rows,
    )
    steps = chip_steps()
    halo_first, halo_second, held, coeffs, own, sent = lax.optimization_barrier(
        (halo_first, halo_second, held, coeffs, own, members)
    )
    fetched = band_swap(sent, sent)

    inc_shape = jax.ShapeDtypeStruct((lev_count, rows, lon_cells), jnp.float32)
    line_shape = jax.ShapeDtypeStruct((lines, lon_cells), jnp.float32)
    chunks = lon_cells // LANES
    chunk_shape = jax.ShapeDtypeStruct((chunks, lines, LANES), jnp.float32)
    halo_shape = jax.ShapeDtypeStruct((chunks, halo_first.shape[0], LANES), jnp.float32)
    zonal_flops = 2 * lines * lon_cells * lon_cells
    chunk_scratch = pltpu.VMEM((chunks, lines, LANES), jnp.float32)
    weighted_scratch = pltpu.VMEM((2 * lines, lon_cells), jnp.bfloat16)
    back_scratch = pltpu.VMEM((chunks, 2 * lines, LANES), jnp.float32)
    def observe(inc, weights, pulls, rims=None):
        if rims is None:
            send_shape = jax.ShapeDtypeStruct((4, lev_count, lon_cells), jnp.float32)
            sends = call(pack_kernel, (flags, inc, weights, pulls), [send_shape, send_shape], [], 0)
            edges = rims = band_swap(*sends)
        else:
            edges = band_swap(*by_partner(inc[None, :, 0], inc[None, :, -1]))
        (adjoint,) = call(
            observe_kernel,
            (flags, inc, *edges, weights, pulls, *rims),
            [jax.ShapeDtypeStruct(inc.shape, jnp.float32)],
            [],
            40 * 2 * inc.size,
        )
        return adjoint, rims

    def opening(held, coeffs, own, halo_first, halo_second):
        held = [held]
        for perm in steps[:-1]:
            held = held + [lax.ppermute(x, "mem", perm) for x in held]
        got = [lax.ppermute(x, "mem", steps[-1]) for x in held]
        mine, other, below, above = call(
            forward_kernel,
            (flags, coeffs, own, halo_first, halo_second, zonal_loc, members),
            [inc_shape, inc_shape, halo_shape, halo_shape],
            [chunk_scratch, pltpu.VMEM(members.shape, members.dtype), pltpu.SemaphoreType.DMA],
            zonal_flops,
            anywhere=1,
        )
        inc = mine + core_swap(other)
        for number, perm in enumerate(steps):
            inc = inc + lax.ppermute(inc, "mem", perm)
            if number == 0:
                inc, got = lax.optimization_barrier((inc, got))
        weights, pulls = band_fields(held + got, lon_cells)
        weights = weights.reshape(2, 2, lev_count, rows, lon_cells)
        pulls = pulls.reshape(2, lev_count, rows, lon_cells)
        adjoint, rims = observe(inc, weights, pulls)
        return adjoint, weights, pulls, rims, below, above

    operands = (held, coeffs, own, halo_first, halo_second)
    shapes = jax.eval_shape(opening, *operands)
    adjoint, weights, pulls, rims, below, above = lax.cond(
        lax.axis_index("lat") < lax.axis_size("lat"),
        opening,
        lambda *_: jax.tree.map(lambda x: jnp.zeros(x.shape, x.dtype), shapes),
        *operands,
    )
    (adjoint, weights, pulls, rims, below, above, own, coeffs), fetched = lax.optimization_barrier(
        ((adjoint, weights, pulls, rims, below, above, own, coeffs), fetched)
    )
    for iteration in range(ITERS):
        if iteration > 0:
            inc = mine + core_swap(other)
            for perm in steps:
                inc = inc + lax.ppermute(inc, "mem", perm)
            adjoint, _ = observe(inc, weights, pulls, rims)
        first, second = band_swap(adjoint, adjoint)
        adjoint_other = core_swap(adjoint)
        (own_back,) = call(
            own_kernel,
            (flags, zonal_loc, adjoint, adjoint_other, members),
            [chunk_shape],
            [pltpu.VMEM((lines, lon_cells), jnp.bfloat16)],
            zonal_flops,
        )
        first, second, own_back = lax.optimization_barrier((first, second, own_back))
        halves = (first, core_swap(first), second, core_swap(second))
        if iteration + 1 < ITERS:
            mine, other, own = call(
                functools.partial(between_kernel, rows, 1),
                (flags, coeffs, own, below, above, zonal_loc, own_back, *halves, members, *fetched),
                [inc_shape, inc_shape, chunk_shape],
                [weighted_scratch, back_scratch, chunk_scratch],
                3 * zonal_flops,
            )
        else:
            (own,) = call(
                functools.partial(last_kernel, rows, 1, 2 * half_band + 1),
                (flags, coeffs, own, zonal_loc, own_back, *halves, *fetched),
                [line_shape],
                [weighted_scratch, back_scratch, chunk_scratch],
                2 * zonal_flops,
            )
    return own.reshape(alpha.shape)


def solution(mesh):
    in_specs = (
        P("mem", None, None, "lat", None),
        P("mem", None, "lat", None),
        P(),
        P(),
        P("lat", "mem", None),
        P("lat", "mem", None),
        P("lat", "mem", None, None),
        P("lat", "mem", None, None),
        P("lat", "mem", None, None),
    )
    out_specs = P("mem", None, "lat", None)
    return jax.shard_map(body, mesh=mesh, in_specs=in_specs, out_specs=out_specs, check_vma=False)
```

```python
import functools

import jax
import jax.numpy as jnp
import numpy as np
from jax import lax
from jax.experimental import pallas as pl
from jax.experimental.pallas import tpu as pltpu
from jax.sharding import PartitionSpec as P

TLON = 128
ITERS = 2
LANES = 128
OBS_CHUNK = 1024
EVEN, CORE, HAS_FIRST, HAS_SECOND, HAS_BELOW, HAS_ABOVE = range(6)


step_size = 0.3


def band_pairs(second):
    bands, groups = lax.axis_size("lat"), lax.axis_size("mem")
    perm = []
    for group in range(groups):
        for band in range(bands):
            other = ((band + second) ^ 1) - second
            if 0 <= other < bands:
                target = group * bands + other
            else:
                target = (group ^ 1) * bands + band
            perm.append((group * bands + band, target))
    return perm


def band_swap(send_first, send_second):
    axes = ("mem", "lat")
    return (
        lax.ppermute(send_first, axes, band_pairs(0)),
        lax.ppermute(send_second, axes, band_pairs(1)),
    )


def band_sides():
    band = lax.axis_index("lat")
    return band % 2 == 0, band > 0, band < lax.axis_size("lat") - 1


def by_partner(to_prev, to_next):
    even, _, _ = band_sides()
    return jnp.where(even, to_next, to_prev), jnp.where(even, to_prev, to_next)


def core_swap(cells):
    count = lax.axis_size("mem")
    return lax.ppermute(cells, "mem", [(i, i ^ 1) for i in range(count)])


def chip_steps():
    count = lax.axis_size("mem")
    bits = [1 << b for b in range(1, count.bit_length() - 1)]
    return [
        [(i, i ^ bits[(step + i % 2) % len(bits)]) for i in range(count)]
        for step in range(len(bits))
    ]


def core_split(cells):
    core = lax.axis_index("mem") % 2
    half = cells.shape[0] // 2
    mine = lax.dynamic_slice_in_dim(cells, core * half, half, 0)
    other = lax.dynamic_slice_in_dim(cells, (1 - core) * half, half, 0)
    return mine, other


def split_two(x):
    top = x.astype(jnp.bfloat16)
    return top, (x - top.astype(jnp.float32)).astype(jnp.bfloat16)


def tile_kernel(tile_ref, count_ref, row_ref, lane_ref, index_ref, value_ref, weight_ref, out_ref):
    slot = pl.program_id(0)
    count = count_ref[slot]
    half = TLON // 2
    wide = half + 8
    rows = row_ref.shape[0]
    out_ref[...] = jnp.zeros_like(out_ref)
    spots = row_ref[...]
    lanes = lane_ref[...]
    coarse = 2 * lax.broadcasted_iota(jnp.int32, (wide, 1), 0)
    chunk = min(OBS_CHUNK, index_ref.shape[-1])

    def step(part, carry):
        @pl.when(part * chunk < count)
        def _():
            here = pl.ds(pl.multiple_of(part * chunk, chunk), chunk)
            index = index_ref[0, :, here]
            weight = weight_ref[0, :, here]
            place = lax.broadcasted_iota(jnp.int32, (1, chunk), 1) + part * chunk
            weight = jnp.where(place < count, weight, 0.0)
            pull = weight * value_ref[0, :, here]
            high = lax.shift_right_logical(index, TLON.bit_length() - 1)
            low = lax.bitwise_and(index, TLON - 1)
            at_row = jnp.where(spots == high, 1.0, 0.0).astype(jnp.bfloat16)
            contract = (((1,), (1,)), ((), ()))
            total = jnp.zeros((rows, TLON), jnp.float32)
            for piece in split_two(weight):
                at_lane = jnp.where(lanes == low, piece.astype(jnp.float32), 0.0)
                total += lax.dot_general(
                    at_row, at_lane.astype(jnp.bfloat16), contract, preferred_element_type=jnp.float32
                )
            apart = jnp.abs(low - coarse)
            share = jnp.where(apart == 0, 1.0, jnp.where(apart == 1, 0.5, 0.0))
            pulled = jnp.zeros((rows, wide), jnp.float32)
            for piece in split_two(pull):
                at_coarse = share * piece.astype(jnp.float32)
                pulled += lax.dot_general(
                    at_row, at_coarse.astype(jnp.bfloat16), contract, preferred_element_type=jnp.float32
                )
            pulled = jnp.concatenate(
                [pulled, jnp.zeros((rows, TLON - wide), jnp.float32)], axis=1
            )
            groups = out_ref.shape[1]
            step_rows = rows // groups
            for group in range(groups):
                mine = slice(group * step_rows, (group + 1) * step_rows)
                out_ref[0, group, :step_rows] += total[mine]
                out_ref[0, group, step_rows:] += pulled[mine]

        return carry

    lax.fori_loop(0, index_ref.shape[-1] // chunk, step, 0)
    step_rows = rows // out_ref.shape[1]
    marker = jnp.where(count > 0, tile_ref[slot] + 1, 0).astype(jnp.float32)
    lane = lax.broadcasted_iota(jnp.int32, (8, TLON), 1)
    for group in range(out_ref.shape[1]):
        block = out_ref[0, group, step_rows : step_rows + 8]
        out_ref[0, group, step_rows : step_rows + 8] = jnp.where(lane == TLON - 1, marker, block)


def tile_sums(tiles, counts, index, value, weight, var_count, lev_count, row_count):
    slots, length = index.shape
    var, par, lev, row = np.meshgrid(
        np.arange(var_count), np.arange(2), np.arange(lev_count), np.arange(row_count), indexing="ij"
    )
    spot = ((var * lev_count + lev) * row_count + row) * 2 + par
    spot = spot.reshape(-1, 1).astype(np.int32)
    lanes = np.arange(TLON).reshape(2, TLON // 2)
    lanes = (2 * (lanes % (TLON // 2)) + lanes // (TLON // 2)).reshape(-1, 1).astype(np.int32)
    rows = spot.shape[0]
    whole = lambda shape: pl.BlockSpec(shape, lambda s, *_: (0,) * len(shape))
    line = pl.BlockSpec((1, 1, length), lambda s, *_: (s, 0, 0))
    out = (slots, var_count, 2 * rows // var_count, TLON)
    return pl.pallas_call(
        tile_kernel,
        grid_spec=pltpu.PrefetchScalarGridSpec(
            num_scalar_prefetch=2,
            grid=(slots,),
            in_specs=[whole(spot.shape), whole(lanes.shape), line, line, line],
            out_specs=pl.BlockSpec((1,) + out[1:], lambda s, *_: (s, 0, 0, 0)),
        ),
        out_shape=jax.ShapeDtypeStruct(out, jnp.float32),
        compiler_params=pltpu.CompilerParams(vmem_limit_bytes=16 * 2**20),
        cost_estimate=pl.CostEstimate(
            flops=2 * slots * length * rows * 400, bytes_accessed=slots * rows * 1024, transcendentals=0
        ),
    )(
        tiles,
        counts,
        jnp.asarray(spot),
        jnp.asarray(lanes),
        index[:, None],
        value[:, None],
        weight[:, None],
    )


def field_kernel(mark_ref, *refs):
    groups = refs[:-3]
    weight_ref, pull_ref, where_ref = refs[-3:]
    tile_count = where_ref.shape[0]
    half = TLON // 2
    size, rows = groups[0].shape[0], weight_ref.shape[1]

    def note(slot, carry):
        mark = mark_ref[slot]

        @pl.when(mark > 0)
        def _():
            where_ref[mark - 1] = slot

        return carry

    def tile_rows(slot, here):
        at = lax.rem(slot, size)
        out = groups[0][at, here]
        for number in range(1, len(groups)):
            out = jnp.where(slot >= number * size, groups[number][at, here], out)
        return out

    for tile in range(tile_count):
        where_ref[tile] = 0
    lax.fori_loop(0, mark_ref.shape[0], note, 0)
    lane = lax.broadcasted_iota(jnp.int32, (rows, TLON), 1)
    upper, lower = slice(0, rows), slice(rows, 2 * rows)
    for pair in range(tile_count // 2):
        left = where_ref[2 * pair]
        right = where_ref[2 * pair + 1]
        before = where_ref[(2 * pair - 1) % tile_count]
        here = slice(pair * TLON, (pair + 1) * TLON)
        first, second = tile_rows(left, upper), tile_rows(right, upper)
        weight_ref[0, :, here] = jnp.where(lane < half, first, pltpu.roll(second, half, 1))
        weight_ref[1, :, here] = jnp.where(lane < half, pltpu.roll(first, half, 1), second)
        first, second, third = tile_rows(left, lower), tile_rows(right, lower), tile_rows(before, lower)
        pull_ref[:, here] = (
            jnp.where(lane <= half, first, 0.0)
            + jnp.where(lane >= half, pltpu.roll(second, half, 1), 0.0)
            + jnp.where(lane == 0, pltpu.roll(third, half, 1), 0.0)
        )


def band_fields(held, lon_cells):
    rows = held[0].shape[1] // 2
    marks = jnp.concatenate([slots[:, rows, TLON - 1] for slots in held]).astype(jnp.int32)
    vmem = pl.BlockSpec(memory_space=pltpu.VMEM)
    return pl.pallas_call(
        field_kernel,
        in_specs=[pl.BlockSpec(memory_space=pltpu.SMEM)] + [vmem] * len(held),
        out_specs=[vmem, vmem],
        out_shape=[
            jax.ShapeDtypeStruct((2, rows, lon_cells), jnp.float32),
            jax.ShapeDtypeStruct((rows, lon_cells), jnp.float32),
        ],
        scratch_shapes=[pltpu.SMEM((2 * lon_cells // TLON,), jnp.int32)],
        compiler_params=pltpu.CompilerParams(vmem_limit_bytes=16 * 2**20),
        cost_estimate=pl.CostEstimate(
            flops=rows * lon_cells * 8, bytes_accessed=rows * lon_cells * 24, transcendentals=0
        ),
    )(marks, *held)


def observation_slots(tiles, counts, index, value, weight, var_count, lev_count, row_count):
    slots = tile_sums(tiles, counts, index, value, weight, var_count, lev_count, row_count)
    mine, other = core_split(slots.transpose(1, 0, 2, 3))
    return jnp.concatenate([mine[0], core_swap(other)[0]], axis=0)


def pull_columns(weight, odd_weight, cells):
    lon = cells.shape[-1]
    odd = odd_weight * (0.5 * (cells + pltpu.roll(cells, lon - 1, cells.ndim - 1)))
    return weight * cells + 0.5 * (odd + pltpu.roll(odd, 1, cells.ndim - 1))


def observe_kernel(
    flag_ref, inc_ref, first_ref, second_ref, weight_ref, pull_ref, rim_first_ref, rim_second_ref, out_ref, *send_refs
):
    even = flag_ref[EVEN] == 1
    has_below, has_above = flag_ref[HAS_BELOW] == 1, flag_ref[HAS_ABOVE] == 1
    levels, rows, lon = inc_ref.shape
    first, second = first_ref[first_ref.shape[0] - 1], second_ref[second_ref.shape[0] - 1]
    lowest = jnp.concatenate([inc_ref[lev, 0:1] for lev in range(levels)], axis=0)
    highest = jnp.concatenate([inc_ref[lev, rows - 1 : rows] for lev in range(levels)], axis=0)
    below = jnp.where(has_below, jnp.where(even, second, first), lowest)
    above = jnp.where(has_above, jnp.where(even, first, second), highest)
    rim_below = [jnp.where(even, rim_second_ref[i], rim_first_ref[i]) for i in range(3)]
    rim_above = [jnp.where(even, rim_first_ref[i], rim_second_ref[i]) for i in range(3)]
    odd_below = pull_columns(rim_below[0], rim_below[1], 0.75 * below + 0.25 * lowest) - rim_below[2]
    even_above = pull_columns(rim_above[0], rim_above[1], 0.75 * above + 0.25 * highest) - rim_above[2]
    row = lax.broadcasted_iota(jnp.int32, (rows, lon), 0)
    for lev in range(levels):
        cells = inc_ref[lev]
        down = jnp.where(row == 0, below[lev : lev + 1], pltpu.roll(cells, 1, 0))
        up = jnp.where(row == rows - 1, above[lev : lev + 1], pltpu.roll(cells, rows - 1, 0))
        low = pull_columns(weight_ref[0, 0, lev], weight_ref[1, 0, lev], 0.75 * cells + 0.25 * down) - pull_ref[0, lev]
        high = pull_columns(weight_ref[0, 1, lev], weight_ref[1, 1, lev], 0.75 * cells + 0.25 * up) - pull_ref[1, lev]
        from_below = jnp.where(has_below, odd_below[lev : lev + 1], low[0:1])
        from_above = jnp.where(has_above, even_above[lev : lev + 1], high[rows - 1 : rows])
        high_down = jnp.where(row == 0, from_below, pltpu.roll(high, 1, 0))
        low_up = jnp.where(row == rows - 1, from_above, pltpu.roll(low, rows - 1, 0))
        out_ref[lev] = 0.75 * (low + high) + 0.25 * (high_down + low_up)
    for pair in range(levels // 2 if send_refs else 0):
        head, tail = half_rows(out_ref[2 * pair], out_ref[2 * pair + 1])
        send_refs[0][pair] = jnp.where(even, tail, head)
        send_refs[1][pair] = jnp.where(even, head, tail)


def half_rows(one, two):
    half = one.shape[0] // 2
    return jnp.concatenate([one[:half], two[:half]], axis=0), jnp.concatenate([one[half:], two[half:]], axis=0)


def row_groups(lines):
    starts = list(range(0, lines - 7, 8))
    return starts if starts[-1] + 8 == lines else starts + [lines - 8]


def strided(ref, chunk, start, rows):
    return ref[chunk, pl.ds(start, 8, stride=rows), :]


def to_chunks(ref, cells):
    for chunk in range(ref.shape[0]):
        ref[chunk] = cells[:, chunk * LANES : (chunk + 1) * LANES]


def spread_rows(cells, coef_ref, base, taps):
    out = []
    for row in range(len(cells) - taps + 1):
        total = coef_ref[base + row * taps] * cells[row]
        for tap in range(1, taps):
            total += coef_ref[base + row * taps + tap] * cells[row + tap]
        out.append(total)
    return out


def pull_rows(cells, coef_ref, base, taps):
    out = []
    for row in range(len(cells) - taps + 1):
        total = coef_ref[base + row * taps] * cells[row + taps - 1]
        for tap in range(1, taps):
            total += coef_ref[base + row * taps + tap] * cells[row + taps - 1 - tap]
        out.append(total)
    return out


def sum_members(core, spread_ref, zonal_ref, members_ref, mine_ref, other_ref):
    size, _, levels, rows, lon = members_ref.shape
    spread = jnp.concatenate(
        [spread_ref[chunk].astype(jnp.bfloat16) for chunk in range(spread_ref.shape[0])], axis=1
    )
    wide = LANES * 3 if lon % (LANES * 3) == 0 else LANES
    for start in range(0, lon, wide):
        lanes = slice(start, start + wide)
        localized = jnp.dot(spread, zonal_ref[:, lanes], preferred_element_type=jnp.float32)
        localized = localized.reshape(size, levels, rows, wide)
        for var, inc_ref in ((core, mine_ref), (1 - core, other_ref)):
            total = members_ref[0, var, :, :, lanes].astype(jnp.float32) * localized[0]
            for k in range(1, size):
                total += members_ref[k, var, :, :, lanes].astype(jnp.float32) * localized[k]
            inc_ref[:, :, lanes] = total


def edge_kernel(alpha_ref, first_ref, second_ref):
    even = lax.rem(lax.axis_index("lat"), 2) == 0
    lines, rows = alpha_ref.shape[:2]
    half = first_ref.shape[0] // lines

    def step(pair, carry):
        one, two = alpha_ref[2 * pair], alpha_ref[2 * pair + 1]
        here = pl.ds(pl.multiple_of(pair * 2 * half, 8), 2 * half)
        head = jnp.concatenate([one[:half], two[:half]], axis=0)
        tail = jnp.concatenate([one[rows - half :], two[rows - half :]], axis=0)
        first_ref[here, :] = jnp.where(even, tail, head)
        second_ref[here, :] = jnp.where(even, head, tail)
        return carry

    lax.fori_loop(0, lines // 2, step, 0, unroll=2)


def forward_kernel(
    flag_ref,
    coef_ref,
    own_ref,
    first_ref,
    second_ref,
    zonal_ref,
    members_from,
    mine_ref,
    other_ref,
    below_ref,
    above_ref,
    spread_ref,
    members_ref,
    arrived,
):
    copy = pltpu.make_async_copy(members_from, members_ref, arrived)
    copy.start()
    rows = members_ref.shape[3]
    half_band = first_ref.shape[0] * rows // own_ref.shape[1]
    taps = 2 * half_band + 1
    even = flag_ref[EVEN] == 1
    first = jnp.where(flag_ref[HAS_FIRST] == 1, first_ref[...], 0.0)
    second = jnp.where(flag_ref[HAS_SECOND] == 1, second_ref[...], 0.0)
    to_chunks(below_ref, jnp.where(even, second, first))
    to_chunks(above_ref, jnp.where(even, first, second))

    def step(chunk, carry):
        for start in row_groups(own_ref.shape[1] // rows):
            cells = wide_rows(own_ref, below_ref, above_ref, chunk, start, rows, half_band)
            for r, total in enumerate(spread_rows(cells, coef_ref, 0, taps)):
                spread_ref[chunk, pl.ds(start * rows + r, 8, stride=rows), :] = total
        return carry

    lax.fori_loop(0, own_ref.shape[0], step, 0)
    copy.wait()
    sum_members(flag_ref[CORE], spread_ref, zonal_ref, members_ref, mine_ref, other_ref)


def wide_rows(own_ref, below_ref, above_ref, chunk, start, rows, half_band):
    below = [strided(below_ref, chunk, start * half_band + r, half_band) for r in range(half_band)]
    own = [strided(own_ref, chunk, start * rows + r, rows) for r in range(rows)]
    above = [strided(above_ref, chunk, start * half_band + r, half_band) for r in range(half_band)]
    return below + own + above


def weigh(part_ref, core, mine_ref, other_ref, weighted_ref, place, there):
    size, _, levels, rows, lon = part_ref.shape
    flat = levels * rows

    def step(k, carry):
        total = part_ref[k, core].astype(jnp.float32) * mine_ref[...]
        total += part_ref[k, 1 - core].astype(jnp.float32) * other_ref[...]
        if there is not None:
            total = jnp.where(there, total, 0.0)
        at = pl.multiple_of(place + k * flat, 16)
        weighted_ref[pl.ds(at, flat), :] = total.reshape(flat, lon).astype(jnp.bfloat16)
        return carry

    lax.fori_loop(0, size, step, 0)


def zonal_back(weighted_ref, zonal_ref, back_ref, lines):
    lon = zonal_ref.shape[0]
    wide = LANES * 3 if lon % (LANES * 3) == 0 else LANES
    for first in range(0, back_ref.shape[1], lines):
        here = slice(first, first + lines)
        weighted = weighted_ref[here, :]
        for start in range(0, lon, wide):
            back = lax.dot_general(
                weighted,
                zonal_ref[start : start + wide, :],
                (((1,), (1,)), ((), ())),
                preferred_element_type=jnp.float32,
            )
            for part in range(wide // LANES):
                back_ref[start // LANES + part, here, :] = back[:, part * LANES : (part + 1) * LANES]


def own_kernel(flag_ref, zonal_ref, mine_ref, other_ref, members_ref, back_ref, weighted_ref):
    weigh(members_ref, flag_ref[CORE], mine_ref, other_ref, weighted_ref, 0, None)
    zonal_back(weighted_ref, zonal_ref, back_ref, back_ref.shape[1])


def partner_back(flag_ref, zonal_ref, adjoints, partners, weighted_ref, back_ref):
    lines = back_ref.shape[1] // 2
    even, core = flag_ref[EVEN], flag_ref[CORE]
    half = len(partners) // 2
    for number, (place, flag) in enumerate((((even * lines), HAS_FIRST), ((1 - even) * lines, HAS_SECOND))):
        for part_ref in partners[number * half : (number + 1) * half]:
            mine_ref, other_ref = adjoints[2 * number : 2 * number + 2]
            weigh(part_ref, core, mine_ref, other_ref, weighted_ref, place, flag_ref[flag] == 1)
            place += part_ref.shape[0] * part_ref.shape[2] * part_ref.shape[3]
    zonal_back(weighted_ref, zonal_ref, back_ref, lines)


def partner_half_back(flag_ref, zonal_ref, adjoints, partners, weighted_ref, back_ref, wide_ref):
    lines = back_ref.shape[1] // 2
    even, core = flag_ref[EVEN], flag_ref[CORE]
    for number, (place, flag) in enumerate((((even * lines), HAS_FIRST), ((1 - even) * lines, HAS_SECOND))):
        part_ref = partners[number]
        size, _, levels, rows, _ = part_ref.shape
        flat = levels * rows // 2
        for which, ref in enumerate(adjoints[2 * number : 2 * number + 2]):
            for pair in range(levels // 2):
                packed = ref[pair]
                upper, lower = packed[: rows // 2], packed[rows // 2 :]
                wide_ref[which, 2 * pair] = jnp.concatenate([upper, upper], axis=0)
                wide_ref[which, 2 * pair + 1] = jnp.concatenate([lower, lower], axis=0)
        there = flag_ref[flag] == 1
        is_above = even == 1 - number

        def step(k, carry, part_ref=part_ref, place=place, there=there, is_above=is_above):
            total = part_ref[k, core].astype(jnp.float32) * wide_ref[0]
            total += part_ref[k, 1 - core].astype(jnp.float32) * wide_ref[1]
            total = jnp.where(there, total, 0.0)
            kept = []
            for pair in range(levels // 2):
                head, tail = half_rows(total[2 * pair], total[2 * pair + 1])
                kept.append(jnp.where(is_above, head, tail))
            at = pl.multiple_of(place + k * flat, 16)
            weighted_ref[pl.ds(at, flat), :] = jnp.concatenate(kept, axis=0).astype(jnp.bfloat16)
            return carry

        lax.fori_loop(0, size, step, 0)
    zonal_back(weighted_ref, zonal_ref, back_ref, 2 * lines)


def half_back_rows(own_ref, partner_ref, chunk, start, rows):
    half, lines = rows // 2, partner_ref.shape[1] // 2
    below = [strided(partner_ref, chunk, start * half + r, half) for r in range(half)]
    own = [strided(own_ref, chunk, start * rows + r, rows) for r in range(rows)]
    above = [strided(partner_ref, chunk, lines + start * half + r, half) for r in range(half)]
    return below + own + above


def back_rows(own_ref, partner_ref, chunk, start, rows, halo):
    lines = own_ref.shape[1]
    out = []
    for at in range(rows - halo, 2 * rows + halo):
        ref = own_ref if rows <= at < 2 * rows else partner_ref
        out.append(strided(ref, chunk, (lines if at >= 2 * rows else 0) + start * rows + at % rows, rows))
    return out


def between_kernel(rows, parts, *refs):
    flag_ref, coef_ref, own_ref, below_ref, above_ref, zonal_ref, own_back_ref = refs[:7]
    adjoints = refs[7:11]
    members_ref = refs[11]
    partners = refs[12 : 12 + 2 * parts]
    mine_ref, other_ref, current_ref, weighted_ref, back_ref, spread_ref = refs[12 + 2 * parts :]
    lines = own_ref.shape[1]
    half_band = below_ref.shape[1] * rows // lines
    taps = 2 * half_band + 1
    partner_back(flag_ref, zonal_ref, adjoints, partners, weighted_ref, back_ref)

    def step(chunk, carry):
        for start in row_groups(lines // rows):
            back = back_rows(own_back_ref, back_ref, chunk, start, rows, 2 * half_band)
            pulled = pull_rows(back, coef_ref, rows * taps, taps)
            cells = wide_rows(own_ref, below_ref, above_ref, chunk, start, rows, half_band)
            cells = [c - step_size * (c + p) for c, p in zip(cells, pulled)]
            for r in range(rows):
                current_ref[chunk, pl.ds(start * rows + r, 8, stride=rows), :] = cells[half_band + r]
            for r, total in enumerate(spread_rows(cells, coef_ref, 0, taps)):
                spread_ref[chunk, pl.ds(start * rows + r, 8, stride=rows), :] = total
        return carry

    lax.fori_loop(0, own_ref.shape[0], step, 0)
    sum_members(flag_ref[CORE], spread_ref, zonal_ref, members_ref, mine_ref, other_ref)


def last_kernel(rows, parts, taps, *refs):
    flag_ref, coef_ref, own_ref, zonal_ref, own_back_ref = refs[:5]
    adjoints = refs[5:9]
    partners = refs[9 : 9 + 2 * parts]
    out_ref, weighted_ref, back_ref, current_ref, wide_ref = refs[9 + 2 * parts :]
    half_band = taps // 2
    partner_half_back(flag_ref, zonal_ref, adjoints, partners, weighted_ref, back_ref, wide_ref)

    def step(chunk, carry):
        for start in row_groups(own_ref.shape[1] // rows):
            back = half_back_rows(own_back_ref, back_ref, chunk, start, rows)
            for r, pulled in enumerate(pull_rows(back, coef_ref, (rows + half_band) * taps, taps)):
                here = pl.ds(start * rows + r, 8, stride=rows)
                cell = own_ref[chunk, here, :]
                current_ref[chunk, here, :] = cell - step_size * (cell + pulled)
        return carry

    lax.fori_loop(0, own_ref.shape[0], step, 0)
    for chunk in range(own_ref.shape[0]):
        out_ref[:, chunk * LANES : (chunk + 1) * LANES] = current_ref[chunk]


def call(kernel, operands, outs, scratch, flops, anywhere=0, budget=20 * 2**20):
    vmem = pl.BlockSpec(memory_space=pltpu.VMEM)
    moved = sum(int(np.prod(x.shape)) * x.dtype.itemsize for x in list(operands) + list(outs))
    return pl.pallas_call(
        kernel,
        in_specs=[pl.BlockSpec(memory_space=pltpu.SMEM)] + [vmem] * (len(operands) - 1 - anywhere)
        + [pl.BlockSpec(memory_space=pl.ANY)] * anywhere,
        out_specs=[vmem] * len(outs),
        out_shape=list(outs),
        scratch_shapes=list(scratch),
        compiler_params=pltpu.CompilerParams(vmem_limit_bytes=budget),
        cost_estimate=pl.CostEstimate(flops=flops, bytes_accessed=moved, transcendentals=0),
    )(*operands)


def setup_kernel(rows, coef_ref, alpha_ref, out_ref, own_ref):
    to_chunks(own_ref, alpha_ref[...])
    count, taps = coef_ref.shape
    half_band = taps // 2
    first = lax.axis_index("lat") * rows

    def write(place, row, tap, on_grid):
        value = jnp.where(on_grid, coef_ref[jnp.clip(row, 0, count - 1), tap], 0.0)
        out_ref[place] = jnp.full(out_ref.shape[1:], value, jnp.float32)

    def forward(row, carry):
        for tap in range(taps):
            write(row * taps + tap, first + row, tap, True)
        return carry

    def backward(row, carry):
        target = first + row - half_band
        for tap in range(taps):
            source = target + half_band - tap
            on_grid = (target >= 0) & (target < count) & (source >= 0) & (source < count)
            write((rows + row) * taps + tap, source, tap, on_grid)
        return carry

    lax.fori_loop(0, rows, forward, 0)
    lax.fori_loop(0, rows + 2 * half_band, backward, 0)


def setup(merid_coef, own, rows):
    taps = merid_coef.shape[1]
    shape = ((2 * rows + taps - 1) * taps, 8, LANES)
    lines, lon = own.shape
    vmem = pl.BlockSpec(memory_space=pltpu.VMEM)
    return pl.pallas_call(
        functools.partial(setup_kernel, rows),
        in_specs=[pl.BlockSpec(memory_space=pltpu.SMEM), vmem],
        out_specs=[vmem, vmem],
        out_shape=[
            jax.ShapeDtypeStruct(shape, jnp.float32),
            jax.ShapeDtypeStruct((lon // LANES, lines, LANES), jnp.float32),
        ],
        compiler_params=pltpu.CompilerParams(vmem_limit_bytes=8 * 2**20),
        cost_estimate=pl.CostEstimate(flops=0, bytes_accessed=shape[0] * 4096 + 8 * own.size, transcendentals=0),
    )(merid_coef, own)


def pack_kernel(flag_ref, inc_ref, weight_ref, pull_ref, first_ref, second_ref):
    even = flag_ref[EVEN] == 1
    levels, rows, _ = inc_ref.shape

    def line(ref, *place):
        return jnp.concatenate([ref[(*place[:-1], lev, slice(place[-1], place[-1] + 1))] for lev in range(levels)], axis=0)

    for number in range(4):
        if number < 2:
            low, high = line(weight_ref, number, 0, 0), line(weight_ref, number, 1, rows - 1)
        elif number == 2:
            low, high = line(pull_ref, 0, 0), line(pull_ref, 1, rows - 1)
        else:
            low, high = line(inc_ref, 0), line(inc_ref, rows - 1)
        first_ref[number] = jnp.where(even, high, low)
        second_ref[number] = jnp.where(even, low, high)


def body(
    members, alpha, zonal_loc, merid_coef, slot_tile, obs_count, obs_index, obs_value, obs_weight
):
    half_band = merid_coef.shape[1] // 2
    _, var_count, lev_count, rows, lon_cells = members.shape
    slot_count = slot_tile.shape[-1]

    members_per = members.shape[0]
    lines = members_per * lev_count * rows
    even, has_below, has_above = band_sides()
    first_there = jnp.where(even, has_above, has_below)
    second_there = jnp.where(even, has_below, has_above)
    core = lax.axis_index("mem") % 2
    flags = jnp.stack(
        [x.astype(jnp.int32) for x in (even, core, first_there, second_there, has_below, has_above)]
    )

    edge_lines = members_per * lev_count * half_band
    edge_shape = jax.ShapeDtypeStruct((edge_lines, lon_cells), jnp.float32)
    vmem = pl.BlockSpec(memory_space=pltpu.VMEM)
    sends = pl.pallas_call(
        edge_kernel,
        in_specs=[vmem],
        out_specs=[vmem, vmem],
        out_shape=[edge_shape, edge_shape],
        compiler_params=pltpu.CompilerParams(vmem_limit_bytes=8 * 2**20),
        cost_estimate=pl.CostEstimate(flops=0, bytes_accessed=16 * edge_lines * lon_cells, transcendentals=0),
    )(alpha.reshape(-1, rows, lon_cells))
    obs_index, obs_value, obs_weight, sends = lax.optimization_barrier((obs_index, obs_value, obs_weight, sends))
    halo_first, halo_second = band_swap(*sends)
    coeffs, own = setup(merid_coef, alpha.reshape(lines, lon_cells), rows)

    held = observation_slots(
        slot_tile.reshape(-1),
        obs_count.reshape(-1),
        obs_index.reshape(slot_count, -1),
        obs_value.reshape(slot_count, -1),
        obs_weight.reshape(slot_count, -1),
        var_count,
        lev_count,
        rows,
    )
    steps = chip_steps()
    halo_first, halo_second, held, coeffs, own, sent = lax.optimization_barrier(
        (halo_first, halo_second, held, coeffs, own, members)
    )
    fetched = band_swap(sent, sent)

    inc_shape = jax.ShapeDtypeStruct((lev_count, rows, lon_cells), jnp.float32)
    line_shape = jax.ShapeDtypeStruct((lines, lon_cells), jnp.float32)
    chunks = lon_cells // LANES
    chunk_shape = jax.ShapeDtypeStruct((chunks, lines, LANES), jnp.float32)
    halo_shape = jax.ShapeDtypeStruct((chunks, halo_first.shape[0], LANES), jnp.float32)
    zonal_flops = 2 * lines * lon_cells * lon_cells
    chunk_scratch = pltpu.VMEM((chunks, lines, LANES), jnp.float32)
    weighted_scratch = pltpu.VMEM((2 * lines, lon_cells), jnp.bfloat16)
    back_scratch = pltpu.VMEM((chunks, 2 * lines, LANES), jnp.float32)
    def observe(inc, weights, pulls, rims=None):
        if rims is None:
            send_shape = jax.ShapeDtypeStruct((4, lev_count, lon_cells), jnp.float32)
            sends = call(pack_kernel, (flags, inc, weights, pulls), [send_shape, send_shape], [], 0)
            edges = rims = band_swap(*sends)
        else:
            edges = band_swap(*by_partner(inc[None, :, 0], inc[None, :, -1]))
        half_shape = jax.ShapeDtypeStruct((lev_count // 2, rows, lon_cells), jnp.float32)
        out_shapes = [inc_shape] if rims is edges else [inc_shape, half_shape, half_shape]
        adjoint, *sends = call(
            observe_kernel, (flags, inc, *edges, weights, pulls, *rims), out_shapes, [], 40 * 2 * inc.size
        )
        return adjoint, sends or rims

    def opening(held, coeffs, own, halo_first, halo_second):
        held = [held]
        for perm in steps[:-1]:
            held = held + [lax.ppermute(x, "mem", perm) for x in held]
        got = [lax.ppermute(x, "mem", steps[-1]) for x in held]
        mine, other, below, above = call(
            forward_kernel,
            (flags, coeffs, own, halo_first, halo_second, zonal_loc, members),
            [inc_shape, inc_shape, halo_shape, halo_shape],
            [chunk_scratch, pltpu.VMEM(members.shape, members.dtype), pltpu.SemaphoreType.DMA],
            zonal_flops,
            anywhere=1,
        )
        inc = mine + core_swap(other)
        for number, perm in enumerate(steps):
            inc = inc + lax.ppermute(inc, "mem", perm)
            if number == 0:
                inc, got = lax.optimization_barrier((inc, got))
        weights, pulls = band_fields(held + got, lon_cells)
        weights = weights.reshape(2, 2, lev_count, rows, lon_cells)
        pulls = pulls.reshape(2, lev_count, rows, lon_cells)
        adjoint, rims = observe(inc, weights, pulls)
        return adjoint, weights, pulls, rims, below, above

    operands = (held, coeffs, own, halo_first, halo_second)
    shapes = jax.eval_shape(opening, *operands)
    adjoint, weights, pulls, rims, below, above = lax.cond(
        lax.axis_index("lat") < lax.axis_size("lat"),
        opening,
        lambda *_: jax.tree.map(lambda x: jnp.zeros(x.shape, x.dtype), shapes),
        *operands,
    )
    (adjoint, weights, pulls, rims, below, above, own, coeffs), fetched = lax.optimization_barrier(
        ((adjoint, weights, pulls, rims, below, above, own, coeffs), fetched)
    )
    for iteration in range(ITERS):
        if iteration > 0:
            inc = mine + core_swap(other)
            for perm in steps:
                inc = inc + lax.ppermute(inc, "mem", perm)
            adjoint, sends = observe(inc, weights, pulls, rims)
        first, second = band_swap(*((adjoint, adjoint) if iteration == 0 else sends))
        adjoint_other = core_swap(adjoint)
        (own_back,) = call(
            own_kernel,
            (flags, zonal_loc, adjoint, adjoint_other, members),
            [chunk_shape],
            [pltpu.VMEM((lines, lon_cells), jnp.bfloat16)],
            zonal_flops,
        )
        first, second, own_back = lax.optimization_barrier((first, second, own_back))
        halves = (first, core_swap(first), second, core_swap(second))
        if iteration + 1 < ITERS:
            mine, other, own = call(
                functools.partial(between_kernel, rows, 1),
                (flags, coeffs, own, below, above, zonal_loc, own_back, *halves, members, *fetched),
                [inc_shape, inc_shape, chunk_shape],
                [weighted_scratch, back_scratch, chunk_scratch],
                3 * zonal_flops,
            )
        else:
            (own,) = call(
                functools.partial(last_kernel, rows, 1, 2 * half_band + 1),
                (flags, coeffs, own, zonal_loc, own_back, *halves, *fetched),
                [line_shape],
                [
                    pltpu.VMEM((lines, lon_cells), jnp.bfloat16),
                    chunk_scratch,
                    chunk_scratch,
                    pltpu.VMEM((2,) + inc_shape.shape, jnp.float32),
                ],
                zonal_flops,
            )
    return own.reshape(alpha.shape)


def solution(mesh):
    in_specs = (
        P("mem", None, None, "lat", None),
        P("mem", None, "lat", None),
        P(),
        P(),
        P("lat", "mem", None),
        P("lat", "mem", None),
        P("lat", "mem", None, None),
        P("lat", "mem", None, None),
        P("lat", "mem", None, None),
    )
    out_specs = P("mem", None, "lat", None)
    return jax.shard_map(body, mesh=mesh, in_specs=in_specs, out_specs=out_specs, check_vma=False)
```

```python
import functools

import jax
import jax.numpy as jnp
import numpy as np
from jax import lax
from jax.experimental import pallas as pl
from jax.experimental.pallas import tpu as pltpu
from jax.sharding import PartitionSpec as P

TLON = 128
ITERS = 2
LANES = 128
OBS_CHUNK = 1024
EVEN, CORE, HAS_FIRST, HAS_SECOND, HAS_BELOW, HAS_ABOVE = range(6)


step_size = 0.3


def band_pairs(second):
    bands, groups = lax.axis_size("lat"), lax.axis_size("mem")
    perm = []
    for group in range(groups):
        for band in range(bands):
            other = ((band + second) ^ 1) - second
            if 0 <= other < bands:
                target = group * bands + other
            else:
                target = (group ^ 1) * bands + band
            perm.append((group * bands + band, target))
    return perm


def band_swap(send_first, send_second):
    axes = ("mem", "lat")
    return (
        lax.ppermute(send_first, axes, band_pairs(0)),
        lax.ppermute(send_second, axes, band_pairs(1)),
    )


def band_sides():
    band = lax.axis_index("lat")
    return band % 2 == 0, band > 0, band < lax.axis_size("lat") - 1


def by_partner(to_prev, to_next):
    even, _, _ = band_sides()
    return jnp.where(even, to_next, to_prev), jnp.where(even, to_prev, to_next)


def core_swap(cells):
    count = lax.axis_size("mem")
    return lax.ppermute(cells, "mem", [(i, i ^ 1) for i in range(count)])


def chip_steps():
    count = lax.axis_size("mem")
    bits = [1 << b for b in range(1, count.bit_length() - 1)]
    return [
        [(i, i ^ bits[(step + i % 2) % len(bits)]) for i in range(count)]
        for step in range(len(bits))
    ]


def core_split(cells):
    core = lax.axis_index("mem") % 2
    half = cells.shape[0] // 2
    mine = lax.dynamic_slice_in_dim(cells, core * half, half, 0)
    other = lax.dynamic_slice_in_dim(cells, (1 - core) * half, half, 0)
    return mine, other


def split_two(x):
    top = x.astype(jnp.bfloat16)
    return top, (x - top.astype(jnp.float32)).astype(jnp.bfloat16)


def tile_kernel(tile_ref, count_ref, row_ref, lane_ref, index_ref, value_ref, weight_ref, out_ref):
    slot = pl.program_id(0)
    count = count_ref[slot]
    half = TLON // 2
    wide = half + 8
    rows = row_ref.shape[0]
    out_ref[...] = jnp.zeros_like(out_ref)
    spots = row_ref[...]
    lanes = lane_ref[...]
    coarse = 2 * lax.broadcasted_iota(jnp.int32, (wide, 1), 0)
    chunk = min(OBS_CHUNK, index_ref.shape[-1])

    def step(part, carry):
        @pl.when(part * chunk < count)
        def _():
            here = pl.ds(pl.multiple_of(part * chunk, chunk), chunk)
            index = index_ref[0, :, here]
            weight = weight_ref[0, :, here]
            place = lax.broadcasted_iota(jnp.int32, (1, chunk), 1) + part * chunk
            weight = jnp.where(place < count, weight, 0.0)
            pull = weight * value_ref[0, :, here]
            high = lax.shift_right_logical(index, TLON.bit_length() - 1)
            low = lax.bitwise_and(index, TLON - 1)
            at_row = jnp.where(spots == high, 1.0, 0.0).astype(jnp.bfloat16)
            contract = (((1,), (1,)), ((), ()))
            total = jnp.zeros((rows, TLON), jnp.float32)
            for piece in split_two(weight):
                at_lane = jnp.where(lanes == low, piece.astype(jnp.float32), 0.0)
                total += lax.dot_general(
                    at_row, at_lane.astype(jnp.bfloat16), contract, preferred_element_type=jnp.float32
                )
            apart = jnp.abs(low - coarse)
            share = jnp.where(apart == 0, 1.0, jnp.where(apart == 1, 0.5, 0.0))
            pulled = jnp.zeros((rows, wide), jnp.float32)
            for piece in split_two(pull):
                at_coarse = share * piece.astype(jnp.float32)
                pulled += lax.dot_general(
                    at_row, at_coarse.astype(jnp.bfloat16), contract, preferred_element_type=jnp.float32
                )
            pulled = jnp.concatenate(
                [pulled, jnp.zeros((rows, TLON - wide), jnp.float32)], axis=1
            )
            groups = out_ref.shape[1]
            step_rows = rows // groups
            for group in range(groups):
                mine = slice(group * step_rows, (group + 1) * step_rows)
                out_ref[0, group, :step_rows] += total[mine]
                out_ref[0, group, step_rows:] += pulled[mine]

        return carry

    lax.fori_loop(0, index_ref.shape[-1] // chunk, step, 0)
    step_rows = rows // out_ref.shape[1]
    marker = jnp.where(count > 0, tile_ref[slot] + 1, 0).astype(jnp.float32)
    lane = lax.broadcasted_iota(jnp.int32, (8, TLON), 1)
    for group in range(out_ref.shape[1]):
        block = out_ref[0, group, step_rows : step_rows + 8]
        out_ref[0, group, step_rows : step_rows + 8] = jnp.where(lane == TLON - 1, marker, block)


def tile_sums(tiles, counts, index, value, weight, var_count, lev_count, row_count):
    slots, length = index.shape
    var, par, lev, row = np.meshgrid(
        np.arange(var_count), np.arange(2), np.arange(lev_count), np.arange(row_count), indexing="ij"
    )
    spot = ((var * lev_count + lev) * row_count + row) * 2 + par
    spot = spot.reshape(-1, 1).astype(np.int32)
    lanes = np.arange(TLON).reshape(2, TLON // 2)
    lanes = (2 * (lanes % (TLON // 2)) + lanes // (TLON // 2)).reshape(-1, 1).astype(np.int32)
    rows = spot.shape[0]
    whole = lambda shape: pl.BlockSpec(shape, lambda s, *_: (0,) * len(shape))
    line = pl.BlockSpec((1, 1, length), lambda s, *_: (s, 0, 0))
    out = (slots, var_count, 2 * rows // var_count, TLON)
    return pl.pallas_call(
        tile_kernel,
        grid_spec=pltpu.PrefetchScalarGridSpec(
            num_scalar_prefetch=2,
            grid=(slots,),
            in_specs=[whole(spot.shape), whole(lanes.shape), line, line, line],
            out_specs=pl.BlockSpec((1,) + out[1:], lambda s, *_: (s, 0, 0, 0)),
        ),
        out_shape=jax.ShapeDtypeStruct(out, jnp.float32),
        compiler_params=pltpu.CompilerParams(vmem_limit_bytes=16 * 2**20),
        cost_estimate=pl.CostEstimate(
            flops=2 * slots * length * rows * 400, bytes_accessed=slots * rows * 1024, transcendentals=0
        ),
    )(
        tiles,
        counts,
        jnp.asarray(spot),
        jnp.asarray(lanes),
        index[:, None],
        value[:, None],
        weight[:, None],
    )


def field_kernel(mark_ref, *refs):
    groups = refs[:-3]
    weight_ref, pull_ref, where_ref = refs[-3:]
    tile_count = where_ref.shape[0]
    half = TLON // 2
    size, rows = groups[0].shape[0], weight_ref.shape[1]

    def note(slot, carry):
        mark = mark_ref[slot]

        @pl.when(mark > 0)
        def _():
            where_ref[mark - 1] = slot

        return carry

    def tile_rows(slot, here):
        at = lax.rem(slot, size)
        out = groups[0][at, here]
        for number in range(1, len(groups)):
            out = jnp.where(slot >= number * size, groups[number][at, here], out)
        return out

    for tile in range(tile_count):
        where_ref[tile] = 0
    lax.fori_loop(0, mark_ref.shape[0], note, 0)
    lane = lax.broadcasted_iota(jnp.int32, (rows, TLON), 1)
    upper, lower = slice(0, rows), slice(rows, 2 * rows)
    for pair in range(tile_count // 2):
        left = where_ref[2 * pair]
        right = where_ref[2 * pair + 1]
        before = where_ref[(2 * pair - 1) % tile_count]
        here = slice(pair * TLON, (pair + 1) * TLON)
        first, second = tile_rows(left, upper), tile_rows(right, upper)
        weight_ref[0, :, here] = jnp.where(lane < half, first, pltpu.roll(second, half, 1))
        weight_ref[1, :, here] = jnp.where(lane < half, pltpu.roll(first, half, 1), second)
        first, second, third = tile_rows(left, lower), tile_rows(right, lower), tile_rows(before, lower)
        pull_ref[:, here] = (
            jnp.where(lane <= half, first, 0.0)
            + jnp.where(lane >= half, pltpu.roll(second, half, 1), 0.0)
            + jnp.where(lane == 0, pltpu.roll(third, half, 1), 0.0)
        )


def band_fields(held, lon_cells):
    rows = held[0].shape[1] // 2
    marks = jnp.concatenate([slots[:, rows, TLON - 1] for slots in held]).astype(jnp.int32)
    vmem = pl.BlockSpec(memory_space=pltpu.VMEM)
    return pl.pallas_call(
        field_kernel,
        in_specs=[pl.BlockSpec(memory_space=pltpu.SMEM)] + [vmem] * len(held),
        out_specs=[vmem, vmem],
        out_shape=[
            jax.ShapeDtypeStruct((2, rows, lon_cells), jnp.float32),
            jax.ShapeDtypeStruct((rows, lon_cells), jnp.float32),
        ],
        scratch_shapes=[pltpu.SMEM((2 * lon_cells // TLON,), jnp.int32)],
        compiler_params=pltpu.CompilerParams(vmem_limit_bytes=16 * 2**20),
        cost_estimate=pl.CostEstimate(
            flops=rows * lon_cells * 8, bytes_accessed=rows * lon_cells * 24, transcendentals=0
        ),
    )(marks, *held)


def observation_slots(tiles, counts, index, value, weight, var_count, lev_count, row_count):
    slots = tile_sums(tiles, counts, index, value, weight, var_count, lev_count, row_count)
    mine, other = core_split(slots.transpose(1, 0, 2, 3))
    return jnp.concatenate([mine[0], core_swap(other)[0]], axis=0)


def pull_columns(weight, odd_weight, cells):
    lon = cells.shape[-1]
    odd = odd_weight * (0.5 * (cells + pltpu.roll(cells, lon - 1, cells.ndim - 1)))
    return weight * cells + 0.5 * (odd + pltpu.roll(odd, 1, cells.ndim - 1))


def observe_kernel(
    flag_ref, inc_ref, first_ref, second_ref, weight_ref, pull_ref, rim_first_ref, rim_second_ref, out_ref, *send_refs
):
    even = flag_ref[EVEN] == 1
    has_below, has_above = flag_ref[HAS_BELOW] == 1, flag_ref[HAS_ABOVE] == 1
    levels, rows, lon = inc_ref.shape
    first, second = first_ref[first_ref.shape[0] - 1], second_ref[second_ref.shape[0] - 1]
    lowest = jnp.concatenate([inc_ref[lev, 0:1] for lev in range(levels)], axis=0)
    highest = jnp.concatenate([inc_ref[lev, rows - 1 : rows] for lev in range(levels)], axis=0)
    below = jnp.where(has_below, jnp.where(even, second, first), lowest)
    above = jnp.where(has_above, jnp.where(even, first, second), highest)
    rim_below = [jnp.where(even, rim_second_ref[i], rim_first_ref[i]) for i in range(3)]
    rim_above = [jnp.where(even, rim_first_ref[i], rim_second_ref[i]) for i in range(3)]
    odd_below = pull_columns(rim_below[0], rim_below[1], 0.75 * below + 0.25 * lowest) - rim_below[2]
    even_above = pull_columns(rim_above[0], rim_above[1], 0.75 * above + 0.25 * highest) - rim_above[2]
    row = lax.broadcasted_iota(jnp.int32, (rows, lon), 0)
    for lev in range(levels):
        cells = inc_ref[lev]
        down = jnp.where(row == 0, below[lev : lev + 1], pltpu.roll(cells, 1, 0))
        up = jnp.where(row == rows - 1, above[lev : lev + 1], pltpu.roll(cells, rows - 1, 0))
        low = pull_columns(weight_ref[0, 0, lev], weight_ref[1, 0, lev], 0.75 * cells + 0.25 * down) - pull_ref[0, lev]
        high = pull_columns(weight_ref[0, 1, lev], weight_ref[1, 1, lev], 0.75 * cells + 0.25 * up) - pull_ref[1, lev]
        from_below = jnp.where(has_below, odd_below[lev : lev + 1], low[0:1])
        from_above = jnp.where(has_above, even_above[lev : lev + 1], high[rows - 1 : rows])
        high_down = jnp.where(row == 0, from_below, pltpu.roll(high, 1, 0))
        low_up = jnp.where(row == rows - 1, from_above, pltpu.roll(low, rows - 1, 0))
        out_ref[lev] = 0.75 * (low + high) + 0.25 * (high_down + low_up)
    for pair in range(levels // 2 if send_refs else 0):
        head, tail = half_rows(out_ref[2 * pair], out_ref[2 * pair + 1])
        send_refs[0][pair] = jnp.where(even, tail, head)
        send_refs[1][pair] = jnp.where(even, head, tail)


def half_rows(one, two):
    half = one.shape[0] // 2
    return jnp.concatenate([one[:half], two[:half]], axis=0), jnp.concatenate([one[half:], two[half:]], axis=0)


def row_groups(lines):
    starts = list(range(0, lines - 7, 8))
    return starts if starts[-1] + 8 == lines else starts + [lines - 8]


def strided(ref, chunk, start, rows):
    return ref[chunk, pl.ds(start, 8, stride=rows), :]


def to_chunks(ref, cells):
    for chunk in range(ref.shape[0]):
        ref[chunk] = cells[:, chunk * LANES : (chunk + 1) * LANES]


def spread_rows(cells, coef_ref, base, taps):
    out = []
    for row in range(len(cells) - taps + 1):
        total = coef_ref[base + row * taps] * cells[row]
        for tap in range(1, taps):
            total += coef_ref[base + row * taps + tap] * cells[row + tap]
        out.append(total)
    return out


def pull_rows(cells, coef_ref, base, taps):
    out = []
    for row in range(len(cells) - taps + 1):
        total = coef_ref[base + row * taps] * cells[row + taps - 1]
        for tap in range(1, taps):
            total += coef_ref[base + row * taps + tap] * cells[row + taps - 1 - tap]
        out.append(total)
    return out


def sum_members(core, spread_ref, zonal_ref, members_ref, mine_ref, other_ref):
    size, _, levels, rows, lon = members_ref.shape
    spread = jnp.concatenate(
        [spread_ref[chunk].astype(jnp.bfloat16) for chunk in range(spread_ref.shape[0])], axis=1
    )
    wide = LANES * 3 if lon % (LANES * 3) == 0 else LANES
    for start in range(0, lon, wide):
        lanes = slice(start, start + wide)
        localized = jnp.dot(spread, zonal_ref[:, lanes], preferred_element_type=jnp.float32)
        localized = localized.reshape(size, levels, rows, wide)
        for var, inc_ref in ((core, mine_ref), (1 - core, other_ref)):
            total = members_ref[0, var, :, :, lanes].astype(jnp.float32) * localized[0]
            for k in range(1, size):
                total += members_ref[k, var, :, :, lanes].astype(jnp.float32) * localized[k]
            inc_ref[:, :, lanes] = total


def edge_kernel(alpha_ref, first_ref, second_ref):
    even = lax.rem(lax.axis_index("lat"), 2) == 0
    lines, rows = alpha_ref.shape[:2]
    half = first_ref.shape[0] // lines

    def step(pair, carry):
        one, two = alpha_ref[2 * pair], alpha_ref[2 * pair + 1]
        here = pl.ds(pl.multiple_of(pair * 2 * half, 8), 2 * half)
        head = jnp.concatenate([one[:half], two[:half]], axis=0)
        tail = jnp.concatenate([one[rows - half :], two[rows - half :]], axis=0)
        first_ref[here, :] = jnp.where(even, tail, head)
        second_ref[here, :] = jnp.where(even, head, tail)
        return carry

    lax.fori_loop(0, lines // 2, step, 0, unroll=2)


def forward_kernel(
    flag_ref,
    coef_ref,
    own_ref,
    first_ref,
    second_ref,
    zonal_ref,
    members_from,
    mine_ref,
    other_ref,
    below_ref,
    above_ref,
    spread_ref,
    members_ref,
    arrived,
):
    copy = pltpu.make_async_copy(members_from, members_ref, arrived)
    copy.start()
    rows = members_ref.shape[3]
    half_band = first_ref.shape[0] * rows // own_ref.shape[1]
    taps = 2 * half_band + 1
    even = flag_ref[EVEN] == 1
    first = jnp.where(flag_ref[HAS_FIRST] == 1, first_ref[...], 0.0)
    second = jnp.where(flag_ref[HAS_SECOND] == 1, second_ref[...], 0.0)
    to_chunks(below_ref, jnp.where(even, second, first))
    to_chunks(above_ref, jnp.where(even, first, second))

    def step(chunk, carry):
        for start in row_groups(own_ref.shape[1] // rows):
            cells = wide_rows(own_ref, below_ref, above_ref, chunk, start, rows, half_band)
            for r, total in enumerate(spread_rows(cells, coef_ref, 0, taps)):
                spread_ref[chunk, pl.ds(start * rows + r, 8, stride=rows), :] = total
        return carry

    lax.fori_loop(0, own_ref.shape[0], step, 0)
    copy.wait()
    sum_members(flag_ref[CORE], spread_ref, zonal_ref, members_ref, mine_ref, other_ref)


def wide_rows(own_ref, below_ref, above_ref, chunk, start, rows, half_band):
    below = [strided(below_ref, chunk, start * half_band + r, half_band) for r in range(half_band)]
    own = [strided(own_ref, chunk, start * rows + r, rows) for r in range(rows)]
    above = [strided(above_ref, chunk, start * half_band + r, half_band) for r in range(half_band)]
    return below + own + above


def weigh(part_ref, core, mine_ref, other_ref, weighted_ref, place, there):
    size, _, levels, rows, lon = part_ref.shape
    flat = levels * rows

    def step(k, carry):
        total = part_ref[k, core].astype(jnp.float32) * mine_ref[...]
        total += part_ref[k, 1 - core].astype(jnp.float32) * other_ref[...]
        if there is not None:
            total = jnp.where(there, total, 0.0)
        at = pl.multiple_of(place + k * flat, 16)
        weighted_ref[pl.ds(at, flat), :] = total.reshape(flat, lon).astype(jnp.bfloat16)
        return carry

    lax.fori_loop(0, size, step, 0)


def zonal_back(weighted_ref, zonal_ref, back_ref, lines):
    lon = zonal_ref.shape[0]
    wide = LANES * 3 if lon % (LANES * 3) == 0 else LANES
    for first in range(0, back_ref.shape[1], lines):
        here = slice(first, first + lines)
        weighted = weighted_ref[here, :]
        for start in range(0, lon, wide):
            back = lax.dot_general(
                weighted,
                zonal_ref[start : start + wide, :],
                (((1,), (1,)), ((), ())),
                preferred_element_type=jnp.float32,
            )
            for part in range(wide // LANES):
                back_ref[start // LANES + part, here, :] = back[:, part * LANES : (part + 1) * LANES]


def own_kernel(flag_ref, zonal_ref, mine_ref, other_ref, members_ref, back_ref, weighted_ref):
    weigh(members_ref, flag_ref[CORE], mine_ref, other_ref, weighted_ref, 0, None)
    zonal_back(weighted_ref, zonal_ref, back_ref, back_ref.shape[1])


def partner_back(flag_ref, zonal_ref, adjoints, partners, weighted_ref, back_ref):
    lines = back_ref.shape[1] // 2
    even, core = flag_ref[EVEN], flag_ref[CORE]
    half = len(partners) // 2
    for number, (place, flag) in enumerate((((even * lines), HAS_FIRST), ((1 - even) * lines, HAS_SECOND))):
        for part_ref in partners[number * half : (number + 1) * half]:
            mine_ref, other_ref = adjoints[2 * number : 2 * number + 2]
            weigh(part_ref, core, mine_ref, other_ref, weighted_ref, place, flag_ref[flag] == 1)
            place += part_ref.shape[0] * part_ref.shape[2] * part_ref.shape[3]
    zonal_back(weighted_ref, zonal_ref, back_ref, lines)


def partner_half_back(flag_ref, zonal_ref, adjoints, partners, weighted_ref, back_ref, wide_ref):
    lines = back_ref.shape[1] // 2
    even, core = flag_ref[EVEN], flag_ref[CORE]
    for number, (place, flag) in enumerate((((even * lines), HAS_FIRST), ((1 - even) * lines, HAS_SECOND))):
        part_ref = partners[number]
        size, _, levels, rows, _ = part_ref.shape
        flat = levels * rows // 2
        for which, ref in enumerate(adjoints[2 * number : 2 * number + 2]):
            for pair in range(levels // 2):
                packed = ref[pair]
                upper, lower = packed[: rows // 2], packed[rows // 2 :]
                wide_ref[which, 2 * pair] = jnp.concatenate([upper, upper], axis=0)
                wide_ref[which, 2 * pair + 1] = jnp.concatenate([lower, lower], axis=0)
        there = flag_ref[flag] == 1
        is_above = even == 1 - number

        def step(k, carry, part_ref=part_ref, place=place, there=there, is_above=is_above):
            total = part_ref[k, core].astype(jnp.float32) * wide_ref[0]
            total += part_ref[k, 1 - core].astype(jnp.float32) * wide_ref[1]
            total = jnp.where(there, total, 0.0)
            kept = []
            for pair in range(levels // 2):
                head, tail = half_rows(total[2 * pair], total[2 * pair + 1])
                kept.append(jnp.where(is_above, head, tail))
            at = pl.multiple_of(place + k * flat, 16)
            weighted_ref[pl.ds(at, flat), :] = jnp.concatenate(kept, axis=0).astype(jnp.bfloat16)
            return carry

        lax.fori_loop(0, size, step, 0)
    zonal_back(weighted_ref, zonal_ref, back_ref, 2 * lines)


def half_back_rows(own_ref, partner_ref, chunk, start, rows):
    half, lines = rows // 2, partner_ref.shape[1] // 2
    below = [strided(partner_ref, chunk, start * half + r, half) for r in range(half)]
    own = [strided(own_ref, chunk, start * rows + r, rows) for r in range(rows)]
    above = [strided(partner_ref, chunk, lines + start * half + r, half) for r in range(half)]
    return below + own + above


def back_rows(own_ref, partner_ref, chunk, start, rows, halo):
    lines = own_ref.shape[1]
    out = []
    for at in range(rows - halo, 2 * rows + halo):
        ref = own_ref if rows <= at < 2 * rows else partner_ref
        out.append(strided(ref, chunk, (lines if at >= 2 * rows else 0) + start * rows + at % rows, rows))
    return out


def between_kernel(rows, parts, *refs):
    flag_ref, coef_ref, own_ref, below_ref, above_ref, zonal_ref, own_back_ref = refs[:7]
    adjoints = refs[7:11]
    members_ref = refs[11]
    partners = refs[12 : 12 + 2 * parts]
    mine_ref, other_ref, current_ref, weighted_ref, back_ref, spread_ref = refs[12 + 2 * parts :]
    lines = own_ref.shape[1]
    half_band = below_ref.shape[1] * rows // lines
    taps = 2 * half_band + 1
    partner_back(flag_ref, zonal_ref, adjoints, partners, weighted_ref, back_ref)

    def step(chunk, carry):
        for start in row_groups(lines // rows):
            back = back_rows(own_back_ref, back_ref, chunk, start, rows, 2 * half_band)
            pulled = pull_rows(back, coef_ref, rows * taps, taps)
            cells = wide_rows(own_ref, below_ref, above_ref, chunk, start, rows, half_band)
            cells = [c - step_size * (c + p) for c, p in zip(cells, pulled)]
            for r in range(rows):
                current_ref[chunk, pl.ds(start * rows + r, 8, stride=rows), :] = cells[half_band + r]
            for r, total in enumerate(spread_rows(cells, coef_ref, 0, taps)):
                spread_ref[chunk, pl.ds(start * rows + r, 8, stride=rows), :] = total
        return carry

    lax.fori_loop(0, own_ref.shape[0], step, 0)
    sum_members(flag_ref[CORE], spread_ref, zonal_ref, members_ref, mine_ref, other_ref)


def last_kernel(rows, parts, taps, *refs):
    flag_ref, coef_ref, own_ref, zonal_ref, own_back_ref = refs[:5]
    adjoints = refs[5:9]
    partners = refs[9 : 9 + 2 * parts]
    out_ref, weighted_ref, back_ref, current_ref, wide_ref, sent = refs[9 + 2 * parts :]
    half_band = taps // 2
    partner_half_back(flag_ref, zonal_ref, adjoints, partners, weighted_ref, back_ref, wide_ref)

    def step(chunk, carry):
        for start in row_groups(own_ref.shape[1] // rows):
            back = half_back_rows(own_back_ref, back_ref, chunk, start, rows)
            for r, pulled in enumerate(pull_rows(back, coef_ref, (rows + half_band) * taps, taps)):
                here = pl.ds(start * rows + r, 8, stride=rows)
                cell = own_ref[chunk, here, :]
                current_ref[chunk, here, :] = cell - step_size * (cell + pulled)
        out_copy(chunk).start()
        return carry

    def out_copy(chunk):
        lanes = pl.ds(pl.multiple_of(chunk * LANES, LANES), LANES)
        return pltpu.make_async_copy(current_ref.at[chunk], out_ref.at[:, lanes], sent.at[chunk])

    lax.fori_loop(0, own_ref.shape[0], step, 0)
    for chunk in range(own_ref.shape[0]):
        out_copy(chunk).wait()


def call(kernel, operands, outs, scratch, flops, anywhere=0, out_anywhere=False, budget=20 * 2**20):
    vmem = pl.BlockSpec(memory_space=pltpu.VMEM)
    moved = sum(int(np.prod(x.shape)) * x.dtype.itemsize for x in list(operands) + list(outs))
    return pl.pallas_call(
        kernel,
        in_specs=[pl.BlockSpec(memory_space=pltpu.SMEM)] + [vmem] * (len(operands) - 1 - anywhere)
        + [pl.BlockSpec(memory_space=pl.ANY)] * anywhere,
        out_specs=[pl.BlockSpec(memory_space=pl.ANY) if out_anywhere else vmem] * len(outs),
        out_shape=list(outs),
        scratch_shapes=list(scratch),
        compiler_params=pltpu.CompilerParams(vmem_limit_bytes=budget),
        cost_estimate=pl.CostEstimate(flops=flops, bytes_accessed=moved, transcendentals=0),
    )(*operands)


def setup_kernel(rows, coef_ref, alpha_ref, out_ref, own_ref):
    to_chunks(own_ref, alpha_ref[...])
    count, taps = coef_ref.shape
    half_band = taps // 2
    first = lax.axis_index("lat") * rows

    def write(place, row, tap, on_grid):
        value = jnp.where(on_grid, coef_ref[jnp.clip(row, 0, count - 1), tap], 0.0)
        out_ref[place] = jnp.full(out_ref.shape[1:], value, jnp.float32)

    def forward(row, carry):
        for tap in range(taps):
            write(row * taps + tap, first + row, tap, True)
        return carry

    def backward(row, carry):
        target = first + row - half_band
        for tap in range(taps):
            source = target + half_band - tap
            on_grid = (target >= 0) & (target < count) & (source >= 0) & (source < count)
            write((rows + row) * taps + tap, source, tap, on_grid)
        return carry

    lax.fori_loop(0, rows, forward, 0)
    lax.fori_loop(0, rows + 2 * half_band, backward, 0)


def setup(merid_coef, own, rows):
    taps = merid_coef.shape[1]
    shape = ((2 * rows + taps - 1) * taps, 8, LANES)
    lines, lon = own.shape
    vmem = pl.BlockSpec(memory_space=pltpu.VMEM)
    return pl.pallas_call(
        functools.partial(setup_kernel, rows),
        in_specs=[pl.BlockSpec(memory_space=pltpu.SMEM), vmem],
        out_specs=[vmem, vmem],
        out_shape=[
            jax.ShapeDtypeStruct(shape, jnp.float32),
            jax.ShapeDtypeStruct((lon // LANES, lines, LANES), jnp.float32),
        ],
        compiler_params=pltpu.CompilerParams(vmem_limit_bytes=8 * 2**20),
        cost_estimate=pl.CostEstimate(flops=0, bytes_accessed=shape[0] * 4096 + 8 * own.size, transcendentals=0),
    )(merid_coef, own)


def pack_kernel(flag_ref, inc_ref, weight_ref, pull_ref, first_ref, second_ref):
    even = flag_ref[EVEN] == 1
    levels, rows, _ = inc_ref.shape

    def line(ref, *place):
        return jnp.concatenate([ref[(*place[:-1], lev, slice(place[-1], place[-1] + 1))] for lev in range(levels)], axis=0)

    for number in range(4):
        if number < 2:
            low, high = line(weight_ref, number, 0, 0), line(weight_ref, number, 1, rows - 1)
        elif number == 2:
            low, high = line(pull_ref, 0, 0), line(pull_ref, 1, rows - 1)
        else:
            low, high = line(inc_ref, 0), line(inc_ref, rows - 1)
        first_ref[number] = jnp.where(even, high, low)
        second_ref[number] = jnp.where(even, low, high)


def body(
    members, alpha, zonal_loc, merid_coef, slot_tile, obs_count, obs_index, obs_value, obs_weight
):
    half_band = merid_coef.shape[1] // 2
    _, var_count, lev_count, rows, lon_cells = members.shape
    slot_count = slot_tile.shape[-1]

    members_per = members.shape[0]
    lines = members_per * lev_count * rows
    even, has_below, has_above = band_sides()
    first_there = jnp.where(even, has_above, has_below)
    second_there = jnp.where(even, has_below, has_above)
    core = lax.axis_index("mem") % 2
    flags = jnp.stack(
        [x.astype(jnp.int32) for x in (even, core, first_there, second_there, has_below, has_above)]
    )

    edge_lines = members_per * lev_count * half_band
    edge_shape = jax.ShapeDtypeStruct((edge_lines, lon_cells), jnp.float32)
    vmem = pl.BlockSpec(memory_space=pltpu.VMEM)
    sends = pl.pallas_call(
        edge_kernel,
        in_specs=[vmem],
        out_specs=[vmem, vmem],
        out_shape=[edge_shape, edge_shape],
        compiler_params=pltpu.CompilerParams(vmem_limit_bytes=8 * 2**20),
        cost_estimate=pl.CostEstimate(flops=0, bytes_accessed=16 * edge_lines * lon_cells, transcendentals=0),
    )(alpha.reshape(-1, rows, lon_cells))
    obs_index, obs_value, obs_weight, sends = lax.optimization_barrier((obs_index, obs_value, obs_weight, sends))
    halo_first, halo_second = band_swap(*sends)
    coeffs, own = setup(merid_coef, alpha.reshape(lines, lon_cells), rows)

    held = observation_slots(
        slot_tile.reshape(-1),
        obs_count.reshape(-1),
        obs_index.reshape(slot_count, -1),
        obs_value.reshape(slot_count, -1),
        obs_weight.reshape(slot_count, -1),
        var_count,
        lev_count,
        rows,
    )
    steps = chip_steps()
    halo_first, halo_second, held, coeffs, own, sent = lax.optimization_barrier(
        (halo_first, halo_second, held, coeffs, own, members)
    )
    fetched = band_swap(sent, sent)

    inc_shape = jax.ShapeDtypeStruct((lev_count, rows, lon_cells), jnp.float32)
    line_shape = jax.ShapeDtypeStruct((lines, lon_cells), jnp.float32)
    chunks = lon_cells // LANES
    chunk_shape = jax.ShapeDtypeStruct((chunks, lines, LANES), jnp.float32)
    halo_shape = jax.ShapeDtypeStruct((chunks, halo_first.shape[0], LANES), jnp.float32)
    zonal_flops = 2 * lines * lon_cells * lon_cells
    chunk_scratch = pltpu.VMEM((chunks, lines, LANES), jnp.float32)
    weighted_scratch = pltpu.VMEM((2 * lines, lon_cells), jnp.bfloat16)
    back_scratch = pltpu.VMEM((chunks, 2 * lines, LANES), jnp.float32)
    def observe(inc, weights, pulls, rims=None):
        if rims is None:
            send_shape = jax.ShapeDtypeStruct((4, lev_count, lon_cells), jnp.float32)
            sends = call(pack_kernel, (flags, inc, weights, pulls), [send_shape, send_shape], [], 0)
            edges = rims = band_swap(*sends)
        else:
            edges = band_swap(*by_partner(inc[None, :, 0], inc[None, :, -1]))
        half_shape = jax.ShapeDtypeStruct((lev_count // 2, rows, lon_cells), jnp.float32)
        out_shapes = [inc_shape] if rims is edges else [inc_shape, half_shape, half_shape]
        adjoint, *sends = call(
            observe_kernel, (flags, inc, *edges, weights, pulls, *rims), out_shapes, [], 40 * 2 * inc.size
        )
        return adjoint, sends or rims

    def opening(held, coeffs, own, halo_first, halo_second):
        held = [held]
        for perm in steps[:-1]:
            held = held + [lax.ppermute(x, "mem", perm) for x in held]
        got = [lax.ppermute(x, "mem", steps[-1]) for x in held]
        mine, other, below, above = call(
            forward_kernel,
            (flags, coeffs, own, halo_first, halo_second, zonal_loc, members),
            [inc_shape, inc_shape, halo_shape, halo_shape],
            [chunk_scratch, pltpu.VMEM(members.shape, members.dtype), pltpu.SemaphoreType.DMA],
            zonal_flops,
            anywhere=1,
        )
        inc = mine + core_swap(other)
        for number, perm in enumerate(steps):
            inc = inc + lax.ppermute(inc, "mem", perm)
            if number == 0:
                inc, got = lax.optimization_barrier((inc, got))
        weights, pulls = band_fields(held + got, lon_cells)
        weights = weights.reshape(2, 2, lev_count, rows, lon_cells)
        pulls = pulls.reshape(2, lev_count, rows, lon_cells)
        adjoint, rims = observe(inc, weights, pulls)
        return adjoint, weights, pulls, rims, below, above

    operands = (held, coeffs, own, halo_first, halo_second)
    shapes = jax.eval_shape(opening, *operands)
    adjoint, weights, pulls, rims, below, above = lax.cond(
        lax.axis_index("lat") < lax.axis_size("lat"),
        opening,
        lambda *_: jax.tree.map(lambda x: jnp.zeros(x.shape, x.dtype), shapes),
        *operands,
    )
    (adjoint, weights, pulls, rims, below, above, own, coeffs), fetched = lax.optimization_barrier(
        ((adjoint, weights, pulls, rims, below, above, own, coeffs), fetched)
    )
    for iteration in range(ITERS):
        if iteration > 0:
            inc = mine + core_swap(other)
            for perm in steps:
                inc = inc + lax.ppermute(inc, "mem", perm)
            adjoint, sends = observe(inc, weights, pulls, rims)
        first, second = band_swap(*((adjoint, adjoint) if iteration == 0 else sends))
        adjoint_other = core_swap(adjoint)
        (own_back,) = call(
            own_kernel,
            (flags, zonal_loc, adjoint, adjoint_other, members),
            [chunk_shape],
            [pltpu.VMEM((lines, lon_cells), jnp.bfloat16)],
            zonal_flops,
        )
        first, second, own_back = lax.optimization_barrier((first, second, own_back))
        halves = (first, core_swap(first), second, core_swap(second))
        if iteration + 1 < ITERS:
            mine, other, own = call(
                functools.partial(between_kernel, rows, 1),
                (flags, coeffs, own, below, above, zonal_loc, own_back, *halves, members, *fetched),
                [inc_shape, inc_shape, chunk_shape],
                [weighted_scratch, back_scratch, chunk_scratch],
                3 * zonal_flops,
            )
        else:
            (own,) = call(
                functools.partial(last_kernel, rows, 1, 2 * half_band + 1),
                (flags, coeffs, own, zonal_loc, own_back, *halves, *fetched),
                [line_shape],
                [
                    pltpu.VMEM((lines, lon_cells), jnp.bfloat16),
                    chunk_scratch,
                    chunk_scratch,
                    pltpu.VMEM((2,) + inc_shape.shape, jnp.float32),
                    pltpu.SemaphoreType.DMA((chunks,)),
                ],
                zonal_flops,
                out_anywhere=True,
            )
    return own.reshape(alpha.shape)


def solution(mesh):
    in_specs = (
        P("mem", None, None, "lat", None),
        P("mem", None, "lat", None),
        P(),
        P(),
        P("lat", "mem", None),
        P("lat", "mem", None),
        P("lat", "mem", None, None),
        P("lat", "mem", None, None),
        P("lat", "mem", None, None),
    )
    out_specs = P("mem", None, "lat", None)
    return jax.shard_map(body, mesh=mesh, in_specs=in_specs, out_specs=out_specs, check_vma=False)
```
